32 devices in a mesh: rep: 8 (over y, x, core), grp: 4 (over z).
Axes of the slice: x: 2, y: 2, z: 4, core: 2. Of those that a mesh axis runs over, the one named last changes fastest.
Arguments:
- image_tokens: bfloat16 [8, 580, 384], P('rep', 'grp'), may hold values from -6 to 6
- valid_count: int32 [8], P('rep'), may hold values from 436 to 580
- first_gain: bfloat16 [384], P('grp'), may hold values from 0.5 to 1.5
- first_bias: bfloat16 [384], P('grp'), may hold values from -4 to 4
- heads_weight: bfloat16 [384, 1152], P('grp'), may hold values from -0.3125 to 0.3125
- heads_bias: bfloat16 [768], P('grp'), may hold values from -6 to 6
- mixing_weight: bfloat16 [384, 384], P('grp'), may hold values from -3.5 to 3.5
- mixing_bias: bfloat16 [384], P('grp'), may hold values from -4 to 4
- second_gain: bfloat16 [384], P('grp'), may hold values from 0.5 to 1.5
- second_bias: bfloat16 [384], P('grp'), may hold values from -4 to 4
- expand_weight: bfloat16 [384, 1536], P('grp'), may hold values from -0.3125 to 0.3125
- expand_bias: bfloat16 [1536], P('grp'), may hold values from -6 to 6
- reduce_weight: bfloat16 [1536, 384], P('grp'), may hold values from -0.21875 to 0.21875
- reduce_bias: bfloat16 [384], P('grp'), may hold values from -4 to 4
- output_cotangent: bfloat16 [8, 580, 384], P('rep', 'grp'), may hold values from -6 to 6
Outputs:
- block_output: bfloat16 [8, 580, 384], P('rep', 'grp')
- input_gradient: float32 [8, 580, 384], P('rep', 'grp')
- first_gain_gradient: float32 [384], P('grp')
- first_bias_gradient: float32 [384], P('grp')
- heads_weight_gradient: float32 [384, 1152], P('grp')
- heads_bias_gradient: float32 [768], P('grp')
- mixing_weight_gradient: float32 [384, 384], P('grp')
- mixing_bias_gradient: float32 [384], P('grp')
- second_gain_gradient: float32 [384], P('grp')
- second_bias_gradient: float32 [384], P('grp')
- expand_weight_gradient: float32 [384, 1536], P('grp')
- expand_bias_gradient: float32 [1536], P('grp')
- reduce_weight_gradient: float32 [1536, 384], P('grp')
- reduce_bias_gradient: float32 [384], P('grp')
The draws below stay inside these ranges and needn't reach their ends.
Inputs may be any that keep to these rules, and one draw needn't show every extreme that they name: Image i's first valid_count[i] token slots hold real tokens, the rest are padding.
All inputs are finite; a program needn't handle non-finite values.
Results may differ from the reference program's by a relative error of at most 0.0091.
Values may be sent and summed in bfloat16 or wider, within the bound.
A program may use at most 64 MiB of HBM per device.

```python
import jax
import jax.numpy as jnp
from jax import lax

D = 384
HEADS = 6
HEAD_DIM = 64
FF = 1536
PAD = 580
SPAN = 145
IMAGES = 8


def touch_ends(values, own_key, smallest, high):
    extent = values.shape
    index_at = [jax.random.randint(jax.random.fold_in(own_key, axis), (), 0, extent[axis]) for axis in range(len(extent))]
    values = values.at[tuple(index_at)].set(smallest)
    longest = extent.index(max(extent))
    index_at[longest] = (index_at[longest] + 1) % extent[longest]
    return values.at[tuple(index_at)].set(high)


def block_scale(rng, shape, cuts, least, high):
    gain = 1.0
    for dim, blocks in cuts:
        draws = jax.random.uniform(jax.random.fold_in(jax.random.fold_in(rng, 6), dim), (blocks,), jnp.float32, least / len(cuts), high / len(cuts))
        gain = gain * jnp.repeat(jnp.exp(draws), shape[dim] // blocks).reshape((-1,) + (1,) * (len(shape) - 1 - dim))
    return gain


def scatter_about(rng, extent, deviation, reach, cuts=(), dtype=jnp.bfloat16):
    level = block_scale(rng, extent, cuts, -0.22, 0.18) if cuts else 1.0
    entries = jax.random.normal(rng, extent, jnp.float32) * deviation * level
    return jnp.minimum(jnp.maximum(entries, -reach), reach).astype(dtype)


def setup_inputs(seed: int = 0) -> dict:
    seeds = jax.random.split(jax.random.key(seed), 16)
    return {
        "image_tokens": scatter_about(seeds[0], (IMAGES, PAD, D), 1.0, 6.0, ((0, 8), (1, 4))),
        "valid_count": touch_ends(jax.random.randint(seeds[1], (IMAGES,), PAD - SPAN + 1, PAD + 1), jax.random.fold_in(seeds[1], 1), PAD - SPAN + 1, PAD).astype(jnp.int32),
        "first_gain": jnp.clip(1.0 + 0.1 * jax.random.normal(seeds[2], (D,), jnp.float32), 0.5, 1.5).astype(jnp.bfloat16),
        "first_bias": scatter_about(seeds[3], (D,), 0.3, 4.0, ((0, 4),)),
        "heads_weight": scatter_about(seeds[4], (D, 3 * D), D ** -0.5, 0.3125, ((0, 4),)),
        "heads_bias": scatter_about(seeds[5], (2 * D,), 0.5, 6.0, ((0, 4),)),
        "mixing_weight": scatter_about(seeds[6], (D, D), (max(D // 128, 2)) ** -0.5, 3.5, ((0, 4),)),
        "mixing_bias": scatter_about(seeds[7], (D,), 0.3, 4.0, ((0, 4),)),
        "second_gain": jnp.clip(1.0 + 0.1 * jax.random.normal(seeds[8], (D,), jnp.float32), 0.5, 1.5).astype(jnp.bfloat16),
        "second_bias": scatter_about(seeds[9], (D,), 0.3, 4.0, ((0, 4),)),
        "expand_weight": scatter_about(seeds[10], (D, FF), D ** -0.5, 0.3125, ((0, 4),)),
        "expand_bias": scatter_about(seeds[11], (FF,), 0.5, 6.0, ((0, 4),)),
        "reduce_weight": scatter_about(seeds[12], (FF, D), (FF // 2) ** -0.5, 0.21875, ((0, 4),)),
        "reduce_bias": scatter_about(seeds[13], (D,), 0.3, 4.0, ((0, 4),)),
        "output_cotangent": scatter_about(seeds[14], (IMAGES, PAD, D), 1.0, 6.0, ((0, 8), (1, 4))),
    }


norm_eps = 1e-06
masked_score = -1000000000.0

@jax.custom_vjp
def low(v):
    return lax.optimization_barrier(v.astype(jnp.bfloat16)).astype(jnp.float32)

@jax.custom_vjp
def low_back(v):
    return v

def low_keep(v):
    return (low(v), None)

def low_pass(kept, grad):
    return (grad,)

def back_keep(v):
    return (v, None)

def back_low(kept, grad):
    return (low(grad),)
low.defvjp(low_keep, low_pass)
low_back.defvjp(back_keep, back_low)

def matmul_high(left, right):
    return jnp.dot(left, right, precision=lax.Precision.HIGHEST)

def layer_norm(hidden, gain_vec, bias_vec):
    average = lax.optimization_barrier(jnp.mean(hidden, axis=-1, keepdims=True))
    centered = hidden - average
    variance = lax.optimization_barrier(jnp.mean(centered * centered, axis=-1, keepdims=True))
    return centered * lax.rsqrt(variance + norm_eps) * gain_vec + bias_vec

def one_image(params, tokens, valid):
    first_gain, first_bias, heads_weight, heads_bias, mixing_weight, mixing_bias, second_gain, second_bias, expand_weight, expand_bias, reduce_weight, reduce_bias = params
    normed_one = low(layer_norm(tokens, first_gain, first_bias))
    projected = matmul_high(normed_one, heads_weight)
    query = low_back(low(projected[:, :D] + heads_bias[:D]))
    keys_all = low_back(low(projected[:, D:2 * D]))
    values_all = low_back(low(projected[:, 2 * D:] + heads_bias[D:]))
    query_h = query.reshape(PAD, HEADS, HEAD_DIM)
    keys_h = keys_all.reshape(PAD, HEADS, HEAD_DIM)
    values_h = values_all.reshape(PAD, HEADS, HEAD_DIM)
    scores = jnp.einsum('qhd,khd->hqk', query_h, keys_h, precision=lax.Precision.HIGHEST) * HEAD_DIM ** (-0.5)
    present = jnp.arange(PAD) < valid
    scores = low_back(jnp.where(present[None, None, :], scores, masked_score))
    row_max = lax.optimization_barrier(jnp.max(scores, axis=-1, keepdims=True))
    exp_scores = jnp.exp(scores - row_max)
    attn_prob = low(exp_scores / lax.optimization_barrier(jnp.sum(exp_scores, axis=-1, keepdims=True)))
    mixed = jnp.einsum('hqk,khd->qhd', attn_prob, values_h, precision=lax.Precision.HIGHEST).reshape(PAD, D)
    mixed = low_back(low(mixed))
    after_attn = tokens + low_back(matmul_high(mixed, mixing_weight) + mixing_bias)
    normed_two = low(layer_norm(after_attn, second_gain, second_bias))
    hidden_pre = low_back(matmul_high(normed_two, expand_weight) + expand_bias)
    activated = low(jax.nn.gelu(hidden_pre))
    return after_attn + low_back(matmul_high(activated, reduce_weight) + reduce_bias)

def reference(image_tokens, valid_count, first_gain, first_bias, heads_weight, heads_bias, mixing_weight, mixing_bias, second_gain, second_bias, expand_weight, expand_bias, reduce_weight, reduce_bias, output_cotangent):
    params = tuple((weight_arg.astype(jnp.float32) for weight_arg in (first_gain, first_bias, heads_weight, heads_bias, mixing_weight, mixing_bias, second_gain, second_bias, expand_weight, expand_bias, reduce_weight, reduce_bias)))

    def forward(tokens_all, weights):

        def image_step(paired):
            return jax.checkpoint(one_image)(weights, paired[0], paired[1])
        return lax.map(image_step, (tokens_all, valid_count))
    outputs, pullback = jax.vjp(forward, image_tokens.astype(jnp.float32), params)
    input_gradient, grads = pullback(output_cotangent.astype(jnp.float32))
    return (outputs.astype(jnp.bfloat16), input_gradient, grads[0], grads[1], grads[2], grads[3], grads[4], grads[5], grads[6], grads[7], grads[8], grads[9], grads[10], grads[11])
```

```python
import functools

import jax
import jax.numpy as jnp
from jax import lax
from jax.experimental import pallas as pl
from jax.experimental.pallas import tpu as pltpu
from jax.sharding import PartitionSpec as P

HEADS = 6
HEAD_DIM = 64
ROWS = 16
TEAM = 8

norm_eps = 1e-06
masked_score = -1000000000.0
f32 = jnp.float32
bf16 = jnp.bfloat16
MESH = pl.DeviceIdType.MESH
VMEM = pltpu.VMEM
LIMIT = 56 * 1024 * 1024


def up(count, unit):
    return (count + unit - 1) // unit * unit


def dot_nn(a, b):
    return lax.dot_general(a, b, (((1,), (0,)), ((), ())), preferred_element_type=f32)


def dot_nt(a, b):
    return lax.dot_general(a, b, (((1,), (1,)), ((), ())), preferred_element_type=f32)


def dot_tn(a, b):
    return lax.dot_general(a, b, (((0,), (0,)), ((), ())), preferred_element_type=f32)


def places():
    rep = lax.axis_index("rep")
    z = lax.axis_index("grp")
    core = lax.rem(rep, 2)
    spot = lax.rem(rep // 2, 4)
    base = rep - lax.rem(rep, TEAM)
    return rep, z, core, spot, base


def greet(devices):
    barrier = pltpu.get_barrier_semaphore()
    for device in devices:
        pl.semaphore_signal(barrier, inc=1, device_id=device, device_id_type=MESH)
    pl.semaphore_wait(barrier, len(devices))


def remote(src, dst, send, recv, device):
    copy = pltpu.make_async_remote_copy(
        src_ref=src, dst_ref=dst, send_sem=send, recv_sem=recv,
        device_id=device, device_id_type=MESH,
    )
    return copy


def team_devices():
    rep, z, core, spot, base = places()
    over_z = [(rep, lax.rem(z + d, 4)) for d in (1, 2, 3)]
    plane = [(base + lax.rem(spot + e, 4) * 2 + core, z) for e in (1, 2, 3)]
    twin = (base + spot * 2 + 1 - core, z)
    return over_z, plane, twin


def gather_kernel(
    w_ref, x_ref, s_ref, w_all, x_all, s_all,
    zs, zr, xs, xr, ss, sr, ps, pr, cs, cr, loc,
):
    rep, z, core, spot, base = places()
    over_z, plane, twin = team_devices()
    half = w_ref.shape[0] // 2
    cols = w_ref.shape[1] // 4
    rows = pl.ds(pl.multiple_of(core * half, 16), half)
    part = pl.ds(pl.multiple_of(spot * cols, 128), cols)
    greet(over_z + plane + [twin])
    copies = []
    for d in (1, 2, 3):
        copy = remote(w_ref.at[rows, part], w_all.at[z, rows, part], zs.at[d], zr.at[d], over_z[d - 1])
        copy.start()
        copies.append(copy)
    others = []
    for d in (1, 2, 3):
        a = remote(x_ref, x_all.at[z], xs.at[d], xr.at[d], over_z[d - 1])
        b = remote(s_ref, s_all.at[z], ss.at[d], sr.at[d], over_z[d - 1])
        a.start()
        b.start()
        others += [a, b]
    locals_ = []
    for k, (src, dst) in enumerate(((w_ref, w_all), (x_ref, x_all), (s_ref, s_all))):
        copy = pltpu.make_async_copy(src, dst.at[z], loc.at[k])
        copy.start()
        locals_.append(copy)
    spread = {}
    for d in (1, 2, 3):
        copies[d - 1].wait_recv()
        owner = lax.rem(z + 4 - d, 4)
        for e in (1, 2, 3):
            here = w_all.at[owner, rows, part]
            copy = remote(here, here, ps.at[d * 3 + e - 4], pr.at[d * 3 + e - 4], plane[e - 1])
            copy.start()
            spread[d, e] = copy
    crossed = []
    for d in (1, 2, 3):
        owner = lax.rem(z + 4 - d, 4)
        for e in (1, 2, 3):
            spread[d, e].wait_recv()
        here = w_all.at[owner, rows]
        copy = remote(here, here, cs.at[d], cr.at[d], twin)
        copy.start()
        crossed.append(copy)
    for copy in locals_:
        copy.wait()
    for copy in others:
        copy.wait()
    for copy in copies:
        copy.wait_send()
    for copy in spread.values():
        copy.wait_send()
    for copy in crossed:
        copy.wait()


def gather_call(w, x, s):
    dma = pltpu.SemaphoreType.DMA
    return pl.pallas_call(
        gather_kernel,
        out_shape=[jax.ShapeDtypeStruct((4,) + a.shape, a.dtype) for a in (w, x, s)],
        in_specs=[pl.BlockSpec(memory_space=VMEM)] * 3,
        out_specs=[pl.BlockSpec(memory_space=VMEM)] * 3,
        scratch_shapes=[dma((4,))] * 6 + [dma((9,))] * 2 + [dma((4,))] * 2 + [dma((3,))],
        compiler_params=pltpu.CompilerParams(
            collective_id=0, has_side_effects=True, vmem_limit_bytes=LIMIT
        ),
        name="gather",
    )(w, x, s)


def cot_kernel(m_ref, t_ref, m_all, t_all, ms, mr, ts, tr, loc):
    rep, z, core, spot, base = places()
    over_z, _, _ = team_devices()
    greet(over_z)
    sent = []
    for d in (1, 2, 3):
        a = remote(m_ref, m_all.at[z], ms.at[d], mr.at[d], over_z[d - 1])
        b = remote(t_ref, t_all.at[z], ts.at[d], tr.at[d], over_z[d - 1])
        a.start()
        b.start()
        sent += [a, b]
    c = pltpu.make_async_copy(m_ref, m_all.at[z], loc.at[0])
    e = pltpu.make_async_copy(t_ref, t_all.at[z], loc.at[1])
    c.start()
    e.start()
    c.wait()
    e.wait()
    for copy in sent:
        copy.wait()


def cot_call(m, t):
    dma = pltpu.SemaphoreType.DMA
    return pl.pallas_call(
        cot_kernel,
        out_shape=[jax.ShapeDtypeStruct((4,) + a.shape, a.dtype) for a in (m, t)],
        in_specs=[pl.BlockSpec(memory_space=VMEM)] * 2,
        out_specs=[pl.BlockSpec(memory_space=VMEM)] * 2,
        scratch_shapes=[dma((4,))] * 4 + [dma((2,))],
        compiler_params=pltpu.CompilerParams(
            collective_id=1, has_side_effects=True, vmem_limit_bytes=LIMIT
        ),
        name="cotangents",
    )(m, t)


def sum_kernel(
    g_ref, v_ref, o_ref, ov_ref,
    got1, h, got2, mine, got3, fin, v1, va, v2, vb, v3,
    s1, r1, s2, r2, s3, r3, s4, r4, s5, r5, sv, rv,
):
    rep, z, core, spot, base = places()
    over_z, plane, twin = team_devices()
    half = g_ref.shape[1] // 2
    cols = g_ref.shape[2] // 4
    rows = pl.ds(pl.multiple_of(core * half, 16), half)
    away = pl.ds(pl.multiple_of((1 - core) * half, 16), half)

    def part(index):
        return pl.ds(pl.multiple_of(index * cols, 128), cols)

    greet(over_z + plane + [twin])
    order = (2, 1, 3, 0)
    first = {}
    for d in order:
        to = lax.rem(z + d, 4)
        copy = remote(g_ref.at[to, away], got1.at[d], s1.at[d], r1.at[d], twin)
        copy.start()
        first[d] = copy
    vec = [remote(v_ref, v1, sv.at[0], rv.at[0], twin)]
    vec[0].start()
    second = {}
    for d in order:
        to = lax.rem(z + d, 4)
        first[d].wait_recv()
        h[d] = (g_ref[to, rows, :].astype(f32) + got1[d].astype(f32)).astype(bf16)
        for e in (1, 2, 3):
            there = lax.rem(spot + e, 4)
            copy = remote(h.at[d, :, part(there)], got2.at[d, e - 1],
                          s2.at[d * 3 + e - 1], r2.at[d * 3 + e - 1], plane[e - 1])
            copy.start()
            second[d, e] = copy
    vec[0].wait_recv()
    va[...] = v_ref[...] + v1[...]
    for e in (1, 2, 3):
        copy = remote(va, v2.at[e - 1], sv.at[e], rv.at[e], plane[e - 1])
        copy.start()
        vec.append(copy)
    third = {}
    for d in order:
        total = h[d, :, part(spot)].astype(f32)
        for e in (1, 2, 3):
            second[d, e].wait_recv()
            total += got2[d, e - 1].astype(f32)
        mine[d] = total.astype(bf16)
        if d:
            copy = remote(mine.at[d], got3.at[d], s3.at[d], r3.at[d], over_z[d - 1])
            copy.start()
            third[d] = copy
    for e in (1, 2, 3):
        vec[e].wait_recv()
    vb[...] = va[...] + v2[0] + v2[1] + v2[2]
    for d in (1, 2, 3):
        copy = remote(vb, v3.at[d - 1], sv.at[d + 3], rv.at[d + 3], over_z[d - 1])
        copy.start()
        vec.append(copy)
    total = mine[0].astype(f32)
    for d in (1, 2, 3):
        third[d].wait_recv()
        total += got3[d].astype(f32)
    fin[rows, part(spot)] = total.astype(bf16)
    fourth = []
    for e in (1, 2, 3):
        here = fin.at[rows, part(spot)]
        copy = remote(here, here, s4.at[e], r4.at[e], plane[e - 1])
        copy.start()
        fourth.append(copy)
    for d in (4, 5, 6):
        vec[d].wait_recv()
    ov_ref[...] = vb[...] + v3[0] + v3[1] + v3[2]
    for copy in fourth:
        copy.wait_recv()
    last = remote(fin.at[rows], fin.at[rows], s5.at[0], r5.at[0], twin)
    last.start()
    last.wait_recv()
    o_ref[...] = fin[...].astype(f32)
    last.wait_send()
    for copies in (first, second, third):
        for copy in copies.values():
            copy.wait_send()
    for copy in fourth + vec:
        copy.wait_send()


def sum_call(g, v):
    dma = pltpu.SemaphoreType.DMA
    _, depth, wide = g.shape
    half, cols = depth // 2, wide // 4
    return pl.pallas_call(
        sum_kernel,
        out_shape=[
            jax.ShapeDtypeStruct((depth, wide), f32),
            jax.ShapeDtypeStruct(v.shape, f32),
        ],
        in_specs=[pl.BlockSpec(memory_space=VMEM)] * 2,
        out_specs=[pl.BlockSpec(memory_space=VMEM)] * 2,
        scratch_shapes=[
            VMEM((4, half, wide), bf16),
            VMEM((4, half, wide), bf16),
            VMEM((4, 3, half, cols), bf16),
            VMEM((4, half, cols), bf16),
            VMEM((4, half, cols), bf16),
            VMEM((depth, wide), bf16),
            VMEM(v.shape, f32),
            VMEM(v.shape, f32),
            VMEM((3,) + v.shape, f32),
            VMEM(v.shape, f32),
            VMEM((3,) + v.shape, f32),
            dma((4,)), dma((4,)), dma((12,)), dma((12,)), dma((4,)), dma((4,)),
            dma((4,)), dma((4,)), dma((1,)), dma((1,)), dma((7,)), dma((7,)),
        ],
        compiler_params=pltpu.CompilerParams(
            collective_id=2, has_side_effects=True, vmem_limit_bytes=LIMIT
        ),
        name="gradient_sum",
    )(g, v)


def normed(x):
    average = jnp.mean(x, axis=-1, keepdims=True)
    centered = x - average
    inverse = lax.rsqrt(jnp.mean(centered * centered, axis=-1, keepdims=True) + norm_eps)
    return centered * inverse, inverse


def norm_back(grad, unit, inverse, gain):
    scaled = grad * gain
    return inverse * (
        scaled
        - jnp.mean(scaled, axis=-1, keepdims=True)
        - unit * jnp.mean(scaled * unit, axis=-1, keepdims=True)
    )


def total(x):
    return jnp.sum(x, axis=0, keepdims=True)


def key_present(shape, axis, span, padded, start, valid):
    slot = lax.broadcasted_iota(jnp.int32, shape, axis) + start
    owner = slot // padded
    inside = slot - owner * padded
    return (inside < span) & (owner * span + inside < valid)


def first_kernel(
    span, valid_ref, w_ref, x_all, s_ref, x_ref, oc_ref,
    out_ref, ga_ref, g_ref, v_ref, mc_ref, st_ref, qkv_ref, dq_ref,
    mixed_s, mc_s, prob_s, wr_s,
):
    z = lax.axis_index("grp")
    valid = valid_ref[0]
    n, padded, width = x_all.shape
    depth = w_ref.shape[1]
    hidden = 4 * width
    vec = s_ref[0].astype(f32) + s_ref[1].astype(f32) + s_ref[2].astype(f32) + s_ref[3].astype(f32)
    gain1, bias1, mixb, gain2, bias2, redb = [vec[i : i + 1] for i in range(6)]
    hb_q, hb_v = vec[6:7], vec[7:8]
    expb = jnp.concatenate([vec[8:9], vec[9:10], vec[10:11], vec[11:12]], 1)
    c1, c2, c3 = 3 * width, 4 * width, 8 * width

    w_heads = w_ref[:, :, :c1].reshape(width, c1)
    unit, _ = normed(x_all[...].reshape(n * padded, width).astype(f32))
    low = (unit * gain1 + bias1).astype(bf16)
    proj = dot_nn(low, w_heads)
    qkv_ref[:, :width] = (proj[:, :width] + hb_q).astype(bf16)
    qkv_ref[:, width : 2 * width] = proj[:, width : 2 * width].astype(bf16)
    qkv_ref[:, 2 * width :] = (proj[:, 2 * width :] + hb_v).astype(bf16)
    own = pl.ds(pl.multiple_of(z * padded, 16), padded)
    scale = HEAD_DIM ** (-0.5)
    present = key_present((padded, n * padded), 1, span, padded, 0, valid)
    lses = []
    for head in range(HEADS):
        lo = head * HEAD_DIM
        q = qkv_ref[own, lo : lo + HEAD_DIM]
        k = qkv_ref[:, width + lo : width + lo + HEAD_DIM]
        v = qkv_ref[:, 2 * width + lo : 2 * width + lo + HEAD_DIM]
        scores = jnp.where(present, dot_nt(q, k) * scale, masked_score)
        top = jnp.max(scores, axis=-1, keepdims=True)
        e = jnp.exp(scores - top)
        row = jnp.sum(e, axis=-1, keepdims=True)
        prob = e / row
        prob_s[head] = prob
        lses.append(top + jnp.log(row))
        mixed_s[:, lo : lo + HEAD_DIM] = dot_nn(prob.astype(bf16), v).astype(bf16)
    w_mix = w_ref[:, :, c1:c2].reshape(width, width)
    mixed = mixed_s[...]
    after = x_ref[...].astype(f32) + dot_nn(mixed, w_mix) + mixb
    unit2, inv2 = normed(after)
    low2 = (unit2 * gain2 + bias2).astype(bf16)
    w_exp = w_ref[:, :, c2:c3].reshape(width, hidden)
    pre = dot_nn(low2, w_exp) + expb
    cube = 0.044715
    root = 0.7978845608028654
    t = jnp.tanh(root * (pre + cube * (pre * pre * pre)))
    act = (0.5 * pre * (1.0 + t)).astype(bf16)
    slope = 0.5 * (1.0 + t) + (0.5 * root) * pre * (1.0 - t * t) * (1.0 + (3.0 * cube) * pre * pre)
    for i in range(n):
        for j in range(4):
            lo = i * width + j * depth
            wr_s[lo : lo + depth, :] = w_ref[i, :, c3 + j * width : c3 + (j + 1) * width]
    w_red = wr_s[...]
    out_ref[...] = (after + dot_nn(act, w_red) + redb).astype(bf16)

    oc = oc_ref[...]
    ocf = oc.astype(f32)
    v_ref[...] = jnp.zeros(v_ref.shape, f32)
    v_ref[5:6, :] = total(ocf)
    g_red = dot_tn(act, oc).astype(bf16)
    for i in range(n):
        for j in range(4):
            lo = i * width + j * depth
            g_ref[i, :, c3 + j * width : c3 + (j + 1) * width] = g_red[lo : lo + depth]
    pre_cot = (slope * dot_nt(oc, w_red)).astype(bf16)
    pre_sum = total(pre_cot.astype(f32))
    for i in range(4):
        v_ref[8 + i : 9 + i, :] = pre_sum[:, i * width : (i + 1) * width]
    g_ref[:, :, c2:c3] = dot_tn(low2, pre_cot).astype(bf16).reshape(n, depth, hidden)
    grad2 = dot_nt(pre_cot, w_exp)
    v_ref[3:4, :] = total(grad2 * unit2)
    v_ref[4:5, :] = total(grad2)
    grad_after = ocf + norm_back(grad2, unit2, inv2, gain2)
    ga_ref[...] = grad_after
    attn_cot = grad_after.astype(bf16)
    v_ref[2:3, :] = total(attn_cot.astype(f32))
    g_ref[:, :, c1:c2] = dot_tn(mixed, attn_cot).astype(bf16).reshape(n, depth, width)
    g_ref[:, :, :c1] = jnp.zeros((n, depth, c1), bf16)
    mc_s[...] = dot_nt(attn_cot, w_mix).astype(bf16)
    mc_ref[...] = mc_s[...]
    cols = []
    for head in range(HEADS):
        lo = head * HEAD_DIM
        k = qkv_ref[:, width + lo : width + lo + HEAD_DIM]
        v = qkv_ref[:, 2 * width + lo : 2 * width + lo + HEAD_DIM]
        prob = prob_s[head]
        grad_prob = dot_nt(mc_s[:, lo : lo + HEAD_DIM], v)
        inner = jnp.sum(prob * grad_prob, axis=-1, keepdims=True)
        cols.append(inner)
        score_cot = (prob * (grad_prob - inner)).astype(bf16)
        dq_ref[:, lo : lo + HEAD_DIM] = (dot_nn(score_cot, k) * scale).astype(bf16)
    lane = lax.broadcasted_iota(jnp.int32, (padded, 128), 1)
    stats = jnp.zeros((padded, 128), f32)
    for head in range(HEADS):
        stats = jnp.where(lane == head, lses[head], stats)
        stats = jnp.where(lane == head + 8, cols[head], stats)
    st_ref[...] = stats.T[:ROWS, :]


def first_call(span, valid, w, x_all, s, x, oc):
    n, padded, width = x_all.shape
    shape = jax.ShapeDtypeStruct
    vmem = pl.BlockSpec(memory_space=VMEM)
    return pl.pallas_call(
        functools.partial(first_kernel, span),
        out_shape=[
            shape((padded, width), bf16),
            shape((padded, width), f32),
            shape(w.shape, bf16),
            shape((ROWS, width), f32),
            shape((padded, width), bf16),
            shape((ROWS, padded), f32),
            shape((n * padded, 3 * width), bf16),
            shape((padded, width), bf16),
        ],
        in_specs=[pl.BlockSpec(memory_space=pltpu.SMEM)] + [vmem] * 5,
        out_specs=[vmem] * 8,
        scratch_shapes=[
            VMEM((padded, width), bf16),
            VMEM((padded, width), bf16),
            VMEM((HEADS, padded, n * padded), f32),
            VMEM((4 * width, width), bf16),
        ],
        compiler_params=pltpu.CompilerParams(vmem_limit_bytes=LIMIT),
        name="forward_and_feed_back",
    )(valid, w, x_all, s, x, oc)


def second_kernel(
    span, valid_ref, w_ref, s_ref, x_ref, ga_ref, mc_ref, st_ref, qkv_ref, dq_ref, g_in, v_in,
    ig_ref, g_ref, v_ref, hc_s,
):
    z = lax.axis_index("grp")
    valid = valid_ref[0]
    padded, width = x_ref.shape
    n = mc_ref.shape[0]
    depth = w_ref.shape[1]
    own = pl.ds(pl.multiple_of(z * padded, 16), padded)
    scale = HEAD_DIM ** (-0.5)
    present = key_present((padded, n * padded), 0, span, padded, z * padded, valid)
    hc_s[:, :width] = dq_ref[...]
    for head in range(HEADS):
        lo = head * HEAD_DIM
        q = qkv_ref[:, lo : lo + HEAD_DIM]
        k = qkv_ref[own, width + lo : width + lo + HEAD_DIM]
        v = qkv_ref[own, 2 * width + lo : 2 * width + lo + HEAD_DIM]
        mc = mc_ref[:, :, lo : lo + HEAD_DIM].reshape(n * padded, HEAD_DIM)
        lse = jnp.concatenate([st_ref[i, head : head + 1, :] for i in range(n)], 1)
        inner = jnp.concatenate([st_ref[i, head + 8 : head + 9, :] for i in range(n)], 1)
        prob = jnp.exp(jnp.where(present, dot_nt(k, q) * scale, masked_score) - lse)
        grad_prob = dot_nt(v, mc)
        hc_s[:, 2 * width + lo : 2 * width + lo + HEAD_DIM] = dot_nn(prob.astype(bf16), mc).astype(bf16)
        score_cot = (prob * (grad_prob - inner)).astype(bf16)
        hc_s[:, width + lo : width + lo + HEAD_DIM] = (dot_nn(score_cot, q) * scale).astype(bf16)
    vec = s_ref[0].astype(f32) + s_ref[1].astype(f32) + s_ref[2].astype(f32) + s_ref[3].astype(f32)
    gain1, bias1 = vec[0:1], vec[1:2]
    unit, inverse = normed(x_ref[...].astype(f32))
    low = (unit * gain1 + bias1).astype(bf16)
    hc = hc_s[...]
    v_ref[...] = v_in[...]
    v_ref[6:7, :] = total(hc[:, :width].astype(f32))
    v_ref[7:8, :] = total(hc[:, 2 * width :].astype(f32))
    g_ref[...] = g_in[...]
    g_ref[:, :, : 3 * width] = dot_tn(low, hc).astype(bf16).reshape(n, depth, 3 * width)
    grad = dot_nt(hc, w_ref[:, :, : 3 * width].reshape(width, 3 * width))
    v_ref[0:1, :] = total(grad * unit)
    v_ref[1:2, :] = total(grad)
    ig_ref[...] = ga_ref[...] + norm_back(grad, unit, inverse, gain1)


def second_call(span, valid, w, s, x, ga, mc, st, qkv, dq, g, v):
    padded, width = x.shape
    shape = jax.ShapeDtypeStruct
    vmem = pl.BlockSpec(memory_space=VMEM)
    return pl.pallas_call(
        functools.partial(second_kernel, span),
        out_shape=[shape((padded, width), f32), shape(g.shape, bf16), shape(v.shape, f32)],
        in_specs=[pl.BlockSpec(memory_space=pltpu.SMEM)] + [vmem] * 10,
        out_specs=[vmem] * 3,
        scratch_shapes=[VMEM((padded, 3 * width), bf16)],
        compiler_params=pltpu.CompilerParams(vmem_limit_bytes=LIMIT),
        name="attention_back",
    )(valid, w, s, x, ga, mc, st, qkv, dq, g, v)


def on_device(
    image_tokens, valid_count, first_gain, first_bias, heads_weight, heads_bias,
    mixing_weight, mixing_bias, second_gain, second_bias, expand_weight, expand_bias,
    reduce_weight, reduce_bias, output_cotangent,
):
    _, span, width = image_tokens.shape
    depth = heads_weight.shape[0]
    padded = up(span, 16)
    z = lax.axis_index("grp")

    def pad_rows(x):
        return jnp.pad(x[0], ((0, padded - span), (0, 0)))

    x = pad_rows(image_tokens)
    oc = pad_rows(output_cotangent)
    w = jnp.concatenate(
        [
            heads_weight,
            mixing_weight,
            expand_weight,
            reduce_weight.reshape(4, depth, width).transpose(1, 0, 2).reshape(depth, 4 * width),
        ],
        1,
    )
    ones = jnp.stack([first_gain, first_bias, mixing_bias, second_gain, second_bias, reduce_bias])
    col = jnp.arange(width) // depth == z
    rows6 = jnp.where(col[None, :], jnp.tile(ones, (1, 4)), 0)
    twos = jnp.where(jnp.arange(2 * width) // (2 * depth) == z, jnp.tile(heads_bias, 4), 0)
    fours = jnp.where(jnp.arange(4)[:, None] == z, expand_bias[None, :], 0)
    s = jnp.concatenate(
        [rows6, twos.reshape(2, width), fours, jnp.zeros((ROWS - 12, width), bf16)], 0
    ).astype(bf16)

    w_all, x_all, s_all = gather_call(w, x, s)
    out, ga, g, v, mc, st, qkv, dq = first_call(span, valid_count, w_all, x_all, s_all, x, oc)
    mc_all, st_all = cot_call(mc, st)
    ig, g, v = second_call(span, valid_count, w_all, s_all, x, ga, mc_all, st_all, qkv, dq, g, v)
    g, v = sum_call(g, v)
    teams = lax.axis_size("rep") // TEAM
    if teams > 1:
        g, v = lax.psum((g / TEAM, v / TEAM), "rep")
    six = lax.dynamic_slice(v, (0, z * depth), (6, depth))
    two = lax.dynamic_slice(v[6:8].reshape(2 * width), (z * 2 * depth,), (2 * depth,))
    four = lax.dynamic_slice(v, (8 + z, 0), (1, width))[0]
    c1, c2, c3 = 3 * width, 4 * width, 8 * width
    g_red = g[:, c3:].reshape(depth, 4, width).transpose(1, 0, 2).reshape(4 * depth, width)
    return (
        out[None, :span], ig[None, :span],
        six[0], six[1], g[:, :c1], two, g[:, c1:c2], six[2], six[3], six[4],
        g[:, c2:c3], four, g_red, six[5],
    )


def solution(mesh):
    tokens = P("rep", "grp", None)
    vec, mat = P("grp"), P("grp", None)
    weights = (vec, vec, mat, vec, mat, vec, vec, vec, mat, vec, mat, vec)
    return jax.shard_map(
        on_device,
        mesh=mesh,
        in_specs=(tokens, P("rep")) + weights + (tokens,),
        out_specs=(tokens, tokens) + weights,
        check_vma=False,
    )
```

```python
import functools

import jax
import jax.numpy as jnp
from jax import lax
from jax.experimental import pallas as pl
from jax.experimental.pallas import tpu as pltpu
from jax.sharding import PartitionSpec as P

HEADS = 6
HEAD_DIM = 64
ROWS = 16
TEAM = 8

norm_eps = 1e-06
masked_score = -1000000000.0
f32 = jnp.float32
bf16 = jnp.bfloat16
MESH = pl.DeviceIdType.MESH
VMEM = pltpu.VMEM
LIMIT = 56 * 1024 * 1024


def up(count, unit):
    return (count + unit - 1) // unit * unit


def dot_nn(a, b):
    return lax.dot_general(a, b, (((1,), (0,)), ((), ())), preferred_element_type=f32)


def dot_nt(a, b):
    return lax.dot_general(a, b, (((1,), (1,)), ((), ())), preferred_element_type=f32)


def dot_tn(a, b):
    return lax.dot_general(a, b, (((0,), (0,)), ((), ())), preferred_element_type=f32)


def places():
    rep = lax.axis_index("rep")
    z = lax.axis_index("grp")
    core = lax.rem(rep, 2)
    spot = lax.rem(rep // 2, 4)
    base = rep - lax.rem(rep, TEAM)
    return rep, z, core, spot, base


def greet(devices):
    barrier = pltpu.get_barrier_semaphore()
    for device in devices:
        pl.semaphore_signal(barrier, inc=1, device_id=device, device_id_type=MESH)
    pl.semaphore_wait(barrier, len(devices))


def remote(src, dst, send, recv, device):
    copy = pltpu.make_async_remote_copy(
        src_ref=src, dst_ref=dst, send_sem=send, recv_sem=recv,
        device_id=device, device_id_type=MESH,
    )
    return copy


def team_devices():
    rep, z, core, spot, base = places()
    over_z = [(rep, lax.rem(z + d, 4)) for d in (1, 2, 3)]
    plane = [(base + lax.rem(spot + e, 4) * 2 + core, z) for e in (1, 2, 3)]
    twin = (base + spot * 2 + 1 - core, z)
    return over_z, plane, twin


def gather_kernel(
    wh_ref, wm_ref, we_ref, wr_ref, x_ref, s_ref, w_all, x_all, s_all,
    zs, zr, xs, xr, ss, sr, ps, pr, cs, cr, loc,
):
    rep, z, core, spot, base = places()
    over_z, plane, twin = team_devices()
    half = w_all.shape[1] // 2
    cols = w_all.shape[2] // 4
    rows = pl.ds(pl.multiple_of(core * half, 16), half)
    part = pl.ds(pl.multiple_of(spot * cols, 128), cols)
    depth, width = wm_ref.shape
    c1, c2, c3 = 3 * width, 4 * width, 8 * width
    w_all[z, :, :c1] = wh_ref[...]
    w_all[z, :, c1:c2] = wm_ref[...]
    w_all[z, :, c2:c3] = we_ref[...]
    for j in range(4):
        w_all[z, :, c3 + j * width : c3 + (j + 1) * width] = wr_ref[j * depth : (j + 1) * depth, :]
    greet(over_z + plane + [twin])
    copies = []
    for d in (1, 2, 3):
        copy = remote(w_all.at[z, rows, part], w_all.at[z, rows, part], zs.at[d], zr.at[d], over_z[d - 1])
        copy.start()
        copies.append(copy)
    others = []
    for d in (1, 2, 3):
        a = remote(x_ref, x_all.at[z], xs.at[d], xr.at[d], over_z[d - 1])
        b = remote(s_ref, s_all.at[z], ss.at[d], sr.at[d], over_z[d - 1])
        a.start()
        b.start()
        others += [a, b]
    locals_ = []
    for k, (src, dst) in enumerate(((x_ref, x_all), (s_ref, s_all))):
        copy = pltpu.make_async_copy(src, dst.at[z], loc.at[k])
        copy.start()
        locals_.append(copy)
    spread = {}
    for d in (1, 2, 3):
        copies[d - 1].wait_recv()
        owner = lax.rem(z + 4 - d, 4)
        for e in (1, 2, 3):
            here = w_all.at[owner, rows, part]
            copy = remote(here, here, ps.at[d * 3 + e - 4], pr.at[d * 3 + e - 4], plane[e - 1])
            copy.start()
            spread[d, e] = copy
    crossed = []
    for d in (1, 2, 3):
        owner = lax.rem(z + 4 - d, 4)
        for e in (1, 2, 3):
            spread[d, e].wait_recv()
        here = w_all.at[owner, rows]
        copy = remote(here, here, cs.at[d], cr.at[d], twin)
        copy.start()
        crossed.append(copy)
    for copy in locals_:
        copy.wait()
    for copy in others:
        copy.wait()
    for copy in copies:
        copy.wait_send()
    for copy in spread.values():
        copy.wait_send()
    for copy in crossed:
        copy.wait()


def gather_call(weights, x, s):
    dma = pltpu.SemaphoreType.DMA
    depth, width = weights[1].shape
    return pl.pallas_call(
        gather_kernel,
        out_shape=[
            jax.ShapeDtypeStruct((4, depth, 12 * width), bf16),
            jax.ShapeDtypeStruct((4,) + x.shape, bf16),
            jax.ShapeDtypeStruct((4,) + s.shape, bf16),
        ],
        in_specs=[pl.BlockSpec(memory_space=VMEM)] * 6,
        out_specs=[pl.BlockSpec(memory_space=VMEM)] * 3,
        scratch_shapes=[dma((4,))] * 6 + [dma((9,))] * 2 + [dma((4,))] * 2 + [dma((2,))],
        compiler_params=pltpu.CompilerParams(
            collective_id=0, has_side_effects=True, vmem_limit_bytes=LIMIT
        ),
        name="gather",
    )(*weights, x, s)


class Flow:
    def __init__(self, g, got1, h, got2, mine, got3, fin, s1, r1, s2, r2, s3, r3, s4, r4, s5, r5):
        self.__dict__.update(locals())
        rep, self.z, self.core, self.spot, base = places()
        self.over_z, self.plane, self.twin = team_devices()
        half = g.shape[1] // 2
        self.cols = g.shape[2] // 4
        self.rows = pl.ds(pl.multiple_of(self.core * half, 16), half)
        self.away = pl.ds(pl.multiple_of((1 - self.core) * half, 16), half)
        self.order = (2, 1, 3, 0)
        self.sent = []

    def part(self, index):
        return pl.ds(pl.multiple_of(index * self.cols, 128), self.cols)

    def go(self, *args):
        copy = remote(*args)
        copy.start()
        self.sent.append(copy)
        return copy

    def to_twin(self):
        self.first = {}
        for d in self.order:
            to = lax.rem(self.z + d, 4)
            self.first[d] = self.go(
                self.g.at[to, self.away], self.got1.at[d], self.s1.at[d], self.r1.at[d], self.twin
            )

    def to_plane(self):
        self.second = {}
        for d in self.order:
            to = lax.rem(self.z + d, 4)
            self.first[d].wait_recv()
            both = self.g[to, self.rows, :].astype(f32) + self.got1[d].astype(f32)
            self.h[d] = both.astype(bf16)
            for e in (1, 2, 3):
                there = lax.rem(self.spot + e, 4)
                k = d * 3 + e - 1
                self.second[d, e] = self.go(
                    self.h.at[d, :, self.part(there)], self.got2.at[d, e - 1],
                    self.s2.at[k], self.r2.at[k], self.plane[e - 1],
                )

    def to_group(self):
        self.third = {}
        for d in self.order:
            summed = self.h[d, :, self.part(self.spot)].astype(f32)
            for e in (1, 2, 3):
                self.second[d, e].wait_recv()
                summed += self.got2[d, e - 1].astype(f32)
            self.mine[d] = summed.astype(bf16)
            if d:
                self.third[d] = self.go(
                    self.mine.at[d], self.got3.at[d], self.s3.at[d], self.r3.at[d], self.over_z[d - 1]
                )

    def spread(self):
        summed = self.mine[0].astype(f32)
        for d in (1, 2, 3):
            self.third[d].wait_recv()
            summed += self.got3[d].astype(f32)
        here = (self.rows, self.part(self.spot))
        self.fin[here] = summed.astype(bf16)
        self.fourth = []
        for e in (1, 2, 3):
            self.fourth.append(
                self.go(self.fin.at[here], self.fin.at[here], self.s4.at[e], self.r4.at[e], self.plane[e - 1])
            )

    def cross(self):
        for copy in self.fourth:
            copy.wait_recv()
        self.last = self.go(
            self.fin.at[self.rows], self.fin.at[self.rows], self.s5.at[0], self.r5.at[0], self.twin
        )

    def finish(self):
        self.last.wait_recv()
        for copy in self.sent:
            copy.wait_send()


def flow_scratch(depth, wide):
    dma = pltpu.SemaphoreType.DMA
    half, cols = depth // 2, wide // 4
    return [
        VMEM((4, half, wide), bf16),
        VMEM((4, half, wide), bf16),
        VMEM((4, 3, half, cols), bf16),
        VMEM((4, half, cols), bf16),
        VMEM((4, half, cols), bf16),
    ], [
        dma((4,)), dma((4,)), dma((12,)), dma((12,)), dma((4,)), dma((4,)),
        dma((4,)), dma((4,)), dma((1,)), dma((1,)),
    ]


def normed(x):
    average = jnp.mean(x, axis=-1, keepdims=True)
    centered = x - average
    inverse = lax.rsqrt(jnp.mean(centered * centered, axis=-1, keepdims=True) + norm_eps)
    return centered * inverse, inverse


def norm_back(grad, unit, inverse, gain):
    scaled = grad * gain
    return inverse * (
        scaled
        - jnp.mean(scaled, axis=-1, keepdims=True)
        - unit * jnp.mean(scaled * unit, axis=-1, keepdims=True)
    )


def total(x):
    return jnp.sum(x, axis=0, keepdims=True)


def key_present(shape, axis, span, padded, start, valid):
    slot = lax.broadcasted_iota(jnp.int32, shape, axis) + start
    owner = slot // padded
    inside = slot - owner * padded
    return (inside < span) & (owner * span + inside < valid)


def first_kernel(
    span, valid_ref, w_ref, x_all, s_ref, x_ref, oc_ref,
    out_ref, ga_ref, g_ref, gm_ref, v_ref, mc_ref, st_ref, qkv_ref, dq_ref,
    mixed_s, mc_s, prob_s, wr_s,
):
    z = lax.axis_index("grp")
    valid = valid_ref[0]
    n, padded, width = x_all.shape
    depth = w_ref.shape[1]
    hidden = 4 * width
    vec = s_ref[0].astype(f32) + s_ref[1].astype(f32) + s_ref[2].astype(f32) + s_ref[3].astype(f32)
    gain1, bias1, mixb, gain2, bias2, redb = [vec[i : i + 1] for i in range(6)]
    hb_q, hb_v = vec[6:7], vec[7:8]
    expb = jnp.concatenate([vec[8:9], vec[9:10], vec[10:11], vec[11:12]], 1)
    c1, c2, c3 = 3 * width, 4 * width, 8 * width

    w_heads = w_ref[:, :, :c1].reshape(width, c1)
    unit, _ = normed(x_all[...].reshape(n * padded, width).astype(f32))
    low = (unit * gain1 + bias1).astype(bf16)
    proj = dot_nn(low, w_heads)
    qkv_ref[:, :width] = (proj[:, :width] + hb_q).astype(bf16)
    qkv_ref[:, width : 2 * width] = proj[:, width : 2 * width].astype(bf16)
    qkv_ref[:, 2 * width :] = (proj[:, 2 * width :] + hb_v).astype(bf16)
    own = pl.ds(pl.multiple_of(z * padded, 16), padded)
    scale = HEAD_DIM ** (-0.5)
    present = key_present((padded, n * padded), 1, span, padded, 0, valid)
    lses = []
    for head in range(HEADS):
        lo = head * HEAD_DIM
        q = qkv_ref[own, lo : lo + HEAD_DIM]
        k = qkv_ref[:, width + lo : width + lo + HEAD_DIM]
        v = qkv_ref[:, 2 * width + lo : 2 * width + lo + HEAD_DIM]
        scores = jnp.where(present, dot_nt(q, k) * scale, masked_score)
        top = jnp.max(scores, axis=-1, keepdims=True)
        e = jnp.exp(scores - top)
        row = jnp.sum(e, axis=-1, keepdims=True)
        prob = e / row
        prob_s[head] = prob
        lses.append(top + jnp.log(row))
        mixed_s[:, lo : lo + HEAD_DIM] = dot_nn(prob.astype(bf16), v).astype(bf16)
    w_mix = w_ref[:, :, c1:c2].reshape(width, width)
    mixed = mixed_s[...]
    after = x_ref[...].astype(f32) + dot_nn(mixed, w_mix) + mixb
    unit2, inv2 = normed(after)
    low2 = (unit2 * gain2 + bias2).astype(bf16)
    w_exp = w_ref[:, :, c2:c3].reshape(width, hidden)
    pre = dot_nn(low2, w_exp) + expb
    cube = 0.044715
    root = 0.7978845608028654
    t = jnp.tanh(root * (pre + cube * (pre * pre * pre)))
    act = (0.5 * pre * (1.0 + t)).astype(bf16)
    slope = 0.5 * (1.0 + t) + (0.5 * root) * pre * (1.0 - t * t) * (1.0 + (3.0 * cube) * pre * pre)
    for i in range(n):
        for j in range(4):
            lo = i * width + j * depth
            wr_s[lo : lo + depth, :] = w_ref[i, :, c3 + j * width : c3 + (j + 1) * width]
    w_red = wr_s[...]
    out_ref[...] = (after + dot_nn(act, w_red) + redb).astype(bf16)

    oc = oc_ref[...]
    ocf = oc.astype(f32)
    v_ref[...] = jnp.zeros(v_ref.shape, f32)
    v_ref[5:6, :] = total(ocf)
    g_red = dot_tn(act, oc).astype(bf16)
    for i in range(n):
        for j in range(4):
            lo = i * width + j * depth
            g_ref[i, :, c2 + j * width : c2 + (j + 1) * width] = g_red[lo : lo + depth]
    pre_cot = (slope * dot_nt(oc, w_red)).astype(bf16)
    pre_sum = total(pre_cot.astype(f32))
    for i in range(4):
        v_ref[8 + i : 9 + i, :] = pre_sum[:, i * width : (i + 1) * width]
    g_ref[:, :, :c2] = dot_tn(low2, pre_cot).astype(bf16).reshape(n, depth, hidden)
    grad2 = dot_nt(pre_cot, w_exp)
    v_ref[3:4, :] = total(grad2 * unit2)
    v_ref[4:5, :] = total(grad2)
    grad_after = ocf + norm_back(grad2, unit2, inv2, gain2)
    ga_ref[...] = grad_after
    attn_cot = grad_after.astype(bf16)
    v_ref[2:3, :] = total(attn_cot.astype(f32))
    gm_ref[...] = dot_tn(mixed, attn_cot).astype(bf16).reshape(n, depth, width)
    mc_s[...] = dot_nt(attn_cot, w_mix).astype(bf16)
    mc_ref[...] = mc_s[...]
    cols = []
    for head in range(HEADS):
        lo = head * HEAD_DIM
        k = qkv_ref[:, width + lo : width + lo + HEAD_DIM]
        v = qkv_ref[:, 2 * width + lo : 2 * width + lo + HEAD_DIM]
        prob = prob_s[head]
        grad_prob = dot_nt(mc_s[:, lo : lo + HEAD_DIM], v)
        inner = jnp.sum(prob * grad_prob, axis=-1, keepdims=True)
        cols.append(inner)
        score_cot = (prob * (grad_prob - inner)).astype(bf16)
        dq_ref[:, lo : lo + HEAD_DIM] = (dot_nn(score_cot, k) * scale).astype(bf16)
    lane = lax.broadcasted_iota(jnp.int32, (padded, 128), 1)
    stats = jnp.zeros((padded, 128), f32)
    for head in range(HEADS):
        stats = jnp.where(lane == head, lses[head], stats)
        stats = jnp.where(lane == head + 8, cols[head], stats)
    st_ref[...] = stats.T[:ROWS, :]


def first_call(span, valid, w, x_all, s, x, oc):
    n, padded, width = x_all.shape
    shape = jax.ShapeDtypeStruct
    vmem = pl.BlockSpec(memory_space=VMEM)
    return pl.pallas_call(
        functools.partial(first_kernel, span),
        out_shape=[
            shape((padded, width), bf16),
            shape((padded, width), f32),
            shape((n, w.shape[1], 8 * width), bf16),
            shape((n, w.shape[1], width), bf16),
            shape((ROWS, width), f32),
            shape((padded, width), bf16),
            shape((ROWS, padded), f32),
            shape((n * padded, 3 * width), bf16),
            shape((padded, width), bf16),
        ],
        in_specs=[pl.BlockSpec(memory_space=pltpu.SMEM)] + [vmem] * 5,
        out_specs=[vmem] * 9,
        scratch_shapes=[
            VMEM((padded, width), bf16),
            VMEM((padded, width), bf16),
            VMEM((HEADS, padded, n * padded), f32),
            VMEM((4 * width, width), bf16),
        ],
        compiler_params=pltpu.CompilerParams(vmem_limit_bytes=LIMIT),
        name="forward_and_feed_back",
    )(valid, w, x_all, s, x, oc)


def second_kernel(
    span, valid_ref, w_ref, s_ref, x_ref, ga_ref, mc_in, st_in, qkv_ref, dq_ref, g_in, gm_ref, v_in,
    ig_ref, fa_ref, fb_ref, ov_ref, *scratch,
):
    hc_s, mc_ref, st_ref, gb, v_ref, v1, va, v2, vb, v3, ms, mr, ts, tr, sv, rv = scratch[:16]
    fa = Flow(g_in, *scratch[16:21], fa_ref, *scratch[21:31])
    fb = Flow(gb, *scratch[31:36], fb_ref, *scratch[36:46])
    z = lax.axis_index("grp")
    over_z, plane, twin = team_devices()
    valid = valid_ref[0]
    padded, width = x_ref.shape
    n = mc_ref.shape[0]
    depth = w_ref.shape[1]
    greet(over_z + plane + [twin])
    cots = []
    for d in (1, 2, 3):
        a = remote(mc_in, mc_ref.at[z], ms.at[d], mr.at[d], over_z[d - 1])
        b = remote(st_in, st_ref.at[z], ts.at[d], tr.at[d], over_z[d - 1])
        a.start()
        b.start()
        cots += [a, b]
    fa.to_twin()
    mc_ref[z] = mc_in[...]
    st_ref[z] = st_in[...]
    hc_s[:, :width] = dq_ref[...]
    gb[:, :, 3 * width :] = gm_ref[...]
    vec = s_ref[0].astype(f32) + s_ref[1].astype(f32) + s_ref[2].astype(f32) + s_ref[3].astype(f32)
    gain1, bias1 = vec[0:1], vec[1:2]
    fa.to_plane()
    for copy in cots:
        copy.wait()
    own = pl.ds(pl.multiple_of(z * padded, 16), padded)
    scale = HEAD_DIM ** (-0.5)
    present = key_present((padded, n * padded), 0, span, padded, z * padded, valid)
    for head in range(HEADS):
        lo = head * HEAD_DIM
        q = qkv_ref[:, lo : lo + HEAD_DIM]
        k = qkv_ref[own, width + lo : width + lo + HEAD_DIM]
        v = qkv_ref[own, 2 * width + lo : 2 * width + lo + HEAD_DIM]
        mc = mc_ref[:, :, lo : lo + HEAD_DIM].reshape(n * padded, HEAD_DIM)
        lse = jnp.concatenate([st_ref[i, head : head + 1, :] for i in range(n)], 1)
        inner = jnp.concatenate([st_ref[i, head + 8 : head + 9, :] for i in range(n)], 1)
        prob = jnp.exp(jnp.where(present, dot_nt(k, q) * scale, masked_score) - lse)
        grad_prob = dot_nt(v, mc)
        hc_s[:, 2 * width + lo : 2 * width + lo + HEAD_DIM] = dot_nn(prob.astype(bf16), mc).astype(bf16)
        score_cot = (prob * (grad_prob - inner)).astype(bf16)
        hc_s[:, width + lo : width + lo + HEAD_DIM] = (dot_nn(score_cot, q) * scale).astype(bf16)
    unit, inverse = normed(x_ref[...].astype(f32))
    low = (unit * gain1 + bias1).astype(bf16)
    hc = hc_s[...]
    gb[:, :, : 3 * width] = dot_tn(low, hc).astype(bf16).reshape(n, depth, 3 * width)
    fb.to_twin()
    v_ref[...] = v_in[...]
    v_ref[6:7, :] = total(hc[:, :width].astype(f32))
    v_ref[7:8, :] = total(hc[:, 2 * width :].astype(f32))
    grad = dot_nt(hc, w_ref[:, :, : 3 * width].reshape(width, 3 * width))
    v_ref[0:1, :] = total(grad * unit)
    v_ref[1:2, :] = total(grad)
    vecs = [remote(v_ref, v1, sv.at[0], rv.at[0], twin)]
    vecs[0].start()
    fb.to_plane()
    fa.to_group()
    ig_ref[...] = ga_ref[...] + norm_back(grad, unit, inverse, gain1)
    vecs[0].wait_recv()
    va[...] = v_ref[...] + v1[...]
    for e in (1, 2, 3):
        copy = remote(va, v2.at[e - 1], sv.at[e], rv.at[e], plane[e - 1])
        copy.start()
        vecs.append(copy)
    fb.to_group()
    for e in (1, 2, 3):
        vecs[e].wait_recv()
    vb[...] = va[...] + v2[0] + v2[1] + v2[2]
    for d in (1, 2, 3):
        copy = remote(vb, v3.at[d - 1], sv.at[d + 3], rv.at[d + 3], over_z[d - 1])
        copy.start()
        vecs.append(copy)
    fa.spread()
    fb.spread()
    fa.cross()
    fb.cross()
    for d in (4, 5, 6):
        vecs[d].wait_recv()
    ov_ref[...] = vb[...] + v3[0] + v3[1] + v3[2]
    fa.finish()
    fb.finish()
    for copy in vecs:
        copy.wait_send()


def second_call(span, valid, w, s, x, ga, mc, st, qkv, dq, g, gm, v):
    padded, width = x.shape
    depth = w.shape[1]
    shape = jax.ShapeDtypeStruct
    vmem = pl.BlockSpec(memory_space=VMEM)
    dma = pltpu.SemaphoreType.DMA
    bufs_a, sems_a = flow_scratch(depth, 8 * width)
    bufs_b, sems_b = flow_scratch(depth, 4 * width)
    return pl.pallas_call(
        functools.partial(second_kernel, span),
        out_shape=[
            shape((padded, width), f32), shape((depth, 8 * width), bf16),
            shape((depth, 4 * width), bf16), shape(v.shape, f32),
        ],
        in_specs=[pl.BlockSpec(memory_space=pltpu.SMEM)] + [vmem] * 11,
        out_specs=[vmem] * 4,
        scratch_shapes=[
            VMEM((padded, 3 * width), bf16),
            VMEM((4,) + mc.shape, bf16),
            VMEM((4,) + st.shape, f32),
            VMEM((4, depth, 4 * width), bf16),
            VMEM(v.shape, f32),
            VMEM(v.shape, f32),
            VMEM(v.shape, f32),
            VMEM((3,) + v.shape, f32),
            VMEM(v.shape, f32),
            VMEM((3,) + v.shape, f32),
            dma((4,)), dma((4,)), dma((4,)), dma((4,)), dma((7,)), dma((7,)),
        ] + bufs_a + sems_a + bufs_b + sems_b,
        compiler_params=pltpu.CompilerParams(
            collective_id=1, has_side_effects=True, vmem_limit_bytes=LIMIT
        ),
        name="attention_back_and_sum",
    )(valid, w, s, x, ga, mc, st, qkv, dq, g, gm, v)


def unpack_kernel(a_ref, b_ref, h_ref, m_ref, e_ref, r_ref):
    depth, width = m_ref.shape
    h_ref[...] = b_ref[:, : 3 * width].astype(f32)
    m_ref[...] = b_ref[:, 3 * width :].astype(f32)
    e_ref[...] = a_ref[:, : 4 * width].astype(f32)
    for j in range(4):
        lo = (4 + j) * width
        r_ref[j * depth : (j + 1) * depth, :] = a_ref[:, lo : lo + width].astype(f32)


def unpack_call(a, b):
    depth, width = a.shape[0], a.shape[1] // 8
    shape = jax.ShapeDtypeStruct
    vmem = pl.BlockSpec(memory_space=VMEM)
    return pl.pallas_call(
        unpack_kernel,
        out_shape=[
            shape((depth, 3 * width), f32), shape((depth, width), f32),
            shape((depth, 4 * width), f32), shape((4 * depth, width), f32),
        ],
        in_specs=[vmem] * 2,
        out_specs=[vmem] * 4,
        compiler_params=pltpu.CompilerParams(vmem_limit_bytes=LIMIT),
        name="unpack",
    )(a, b)


def on_device(
    image_tokens, valid_count, first_gain, first_bias, heads_weight, heads_bias,
    mixing_weight, mixing_bias, second_gain, second_bias, expand_weight, expand_bias,
    reduce_weight, reduce_bias, output_cotangent,
):
    _, span, width = image_tokens.shape
    depth = heads_weight.shape[0]
    padded = up(span, 16)
    z = lax.axis_index("grp")

    def pad_rows(x):
        return jnp.pad(x[0], ((0, padded - span), (0, 0)))

    x = pad_rows(image_tokens)
    oc = pad_rows(output_cotangent)
    ones = jnp.stack([first_gain, first_bias, mixing_bias, second_gain, second_bias, reduce_bias])
    col = jnp.arange(width) // depth == z
    rows6 = jnp.where(col[None, :], jnp.tile(ones, (1, 4)), 0)
    twos = jnp.where(jnp.arange(2 * width) // (2 * depth) == z, jnp.tile(heads_bias, 4), 0)
    fours = jnp.where(jnp.arange(4)[:, None] == z, expand_bias[None, :], 0)
    s = jnp.concatenate(
        [rows6, twos.reshape(2, width), fours, jnp.zeros((ROWS - 12, width), bf16)], 0
    ).astype(bf16)

    weights = (heads_weight, mixing_weight, expand_weight, reduce_weight)
    w_all, x_all, s_all = gather_call(weights, x, s)
    out, ga, g, gm, v, mc, st, qkv, dq = first_call(span, valid_count, w_all, x_all, s_all, x, oc)
    ig, ga_sum, gb_sum, v = second_call(
        span, valid_count, w_all, s_all, x, ga, mc, st, qkv, dq, g, gm, v
    )
    teams = lax.axis_size("rep") // TEAM
    if teams > 1:
        ga_sum, gb_sum, v = lax.psum(
            (ga_sum.astype(f32) / TEAM, gb_sum.astype(f32) / TEAM, v / TEAM), "rep"
        )
    g_heads, g_mix, g_exp, g_red = unpack_call(ga_sum, gb_sum)
    six = lax.dynamic_slice(v, (0, z * depth), (6, depth))
    two = lax.dynamic_slice(v[6:8].reshape(2 * width), (z * 2 * depth,), (2 * depth,))
    four = lax.dynamic_slice(v, (8 + z, 0), (1, width))[0]
    return (
        out[None, :span], ig[None, :span],
        six[0], six[1], g_heads, two, g_mix, six[2], six[3], six[4],
        g_exp, four, g_red, six[5],
    )


def solution(mesh):
    tokens = P("rep", "grp", None)
    vec, mat = P("grp"), P("grp", None)
    weights = (vec, vec, mat, vec, mat, vec, vec, vec, mat, vec, mat, vec)
    return jax.shard_map(
        on_device,
        mesh=mesh,
        in_specs=(tokens, P("rep")) + weights + (tokens,),
        out_specs=(tokens, tokens) + weights,
        check_vma=False,
    )
```

```python
import functools

import jax
import jax.numpy as jnp
from jax import lax
from jax.experimental import pallas as pl
from jax.experimental.pallas import tpu as pltpu
from jax.sharding import PartitionSpec as P

HEADS = 6
HEAD_DIM = 64
ROWS = 16
TEAM = 8

norm_eps = 1e-06
masked_score = -1000000000.0
f32 = jnp.float32
bf16 = jnp.bfloat16
MESH = pl.DeviceIdType.MESH
VMEM = pltpu.VMEM
LIMIT = 56 * 1024 * 1024


def up(count, unit):
    return (count + unit - 1) // unit * unit


def dot_nn(a, b):
    return lax.dot_general(a, b, (((1,), (0,)), ((), ())), preferred_element_type=f32)


def dot_nt(a, b):
    return lax.dot_general(a, b, (((1,), (1,)), ((), ())), preferred_element_type=f32)


def dot_tn(a, b):
    return lax.dot_general(a, b, (((0,), (0,)), ((), ())), preferred_element_type=f32)


def places():
    rep = lax.axis_index("rep")
    z = lax.axis_index("grp")
    core = lax.rem(rep, 2)
    spot = lax.rem(rep // 2, 4)
    base = rep - lax.rem(rep, TEAM)
    return rep, z, core, spot, base


def greet(devices):
    barrier = pltpu.get_barrier_semaphore()
    for device in devices:
        pl.semaphore_signal(barrier, inc=1, device_id=device, device_id_type=MESH)
    pl.semaphore_wait(barrier, len(devices))


def remote(src, dst, send, recv, device):
    copy = pltpu.make_async_remote_copy(
        src_ref=src, dst_ref=dst, send_sem=send, recv_sem=recv,
        device_id=device, device_id_type=MESH,
    )
    return copy


def team_devices():
    rep, z, core, spot, base = places()
    over_z = [(rep, lax.rem(z + d, 4)) for d in (1, 2, 3)]
    plane = [(base + lax.rem(spot + e, 4) * 2 + core, z) for e in (1, 2, 3)]
    twin = (base + spot * 2 + 1 - core, z)
    return over_z, plane, twin


class Fetch:
    def __init__(self, w, zs, zr, ps, pr, cs, cr):
        self.__dict__.update(locals())
        rep, self.z, core, spot, base = places()
        self.over_z, self.plane, self.twin = team_devices()
        half, cols = w.shape[1] // 2, w.shape[2] // 4
        self.rows = pl.ds(pl.multiple_of(core * half, 16), half)
        self.part = pl.ds(pl.multiple_of(spot * cols, 128), cols)
        self.sent = []

    def go(self, here, *args):
        copy = remote(here, here, *args)
        copy.start()
        self.sent.append(copy)
        return copy

    def to_group(self):
        self.first = {}
        for d in (1, 2, 3):
            here = self.w.at[self.z, self.rows, self.part]
            self.first[d] = self.go(here, self.zs.at[d], self.zr.at[d], self.over_z[d - 1])

    def to_plane(self):
        self.second = {}
        for d in (1, 2, 3):
            owner = lax.rem(self.z + 4 - d, 4)
            self.first[d].wait_recv()
            for e in (1, 2, 3):
                here = self.w.at[owner, self.rows, self.part]
                k = d * 3 + e - 4
                self.second[d, e] = self.go(here, self.ps.at[k], self.pr.at[k], self.plane[e - 1])

    def to_twin(self):
        self.third = []
        for d in (1, 2, 3):
            owner = lax.rem(self.z + 4 - d, 4)
            for e in (1, 2, 3):
                self.second[d, e].wait_recv()
            here = self.w.at[owner, self.rows]
            self.third.append(self.go(here, self.cs.at[d], self.cr.at[d], self.twin))

    def arrive(self):
        for copy in self.third:
            copy.wait_recv()

    def finish(self):
        for copy in self.sent:
            copy.wait_send()


class Flow:
    def __init__(self, g, got1, h, got2, mine, got3, fin, s1, r1, s2, r2, s3, r3, s4, r4, s5, r5):
        self.__dict__.update(locals())
        rep, self.z, self.core, self.spot, base = places()
        self.over_z, self.plane, self.twin = team_devices()
        half = g.shape[1] // 2
        self.cols = g.shape[2] // 4
        self.rows = pl.ds(pl.multiple_of(self.core * half, 16), half)
        self.away = pl.ds(pl.multiple_of((1 - self.core) * half, 16), half)
        self.order = (2, 1, 3, 0)
        self.sent = []

    def part(self, index):
        return pl.ds(pl.multiple_of(index * self.cols, 128), self.cols)

    def go(self, *args):
        copy = remote(*args)
        copy.start()
        self.sent.append(copy)
        return copy

    def to_twin(self):
        self.first = {}
        for d in self.order:
            to = lax.rem(self.z + d, 4)
            self.first[d] = self.go(
                self.g.at[to, self.away], self.got1.at[d], self.s1.at[d], self.r1.at[d], self.twin
            )

    def to_plane(self):
        self.second = {}
        for d in self.order:
            to = lax.rem(self.z + d, 4)
            self.first[d].wait_recv()
            both = self.g[to, self.rows, :].astype(f32) + self.got1[d].astype(f32)
            self.h[d] = both.astype(bf16)
            for e in (1, 2, 3):
                there = lax.rem(self.spot + e, 4)
                k = d * 3 + e - 1
                self.second[d, e] = self.go(
                    self.h.at[d, :, self.part(there)], self.got2.at[d, e - 1],
                    self.s2.at[k], self.r2.at[k], self.plane[e - 1],
                )

    def to_group(self):
        self.third = {}
        for d in self.order:
            summed = self.h[d, :, self.part(self.spot)].astype(f32)
            for e in (1, 2, 3):
                self.second[d, e].wait_recv()
                summed += self.got2[d, e - 1].astype(f32)
            self.mine[d] = summed.astype(bf16)
            if d:
                self.third[d] = self.go(
                    self.mine.at[d], self.got3.at[d], self.s3.at[d], self.r3.at[d], self.over_z[d - 1]
                )

    def spread(self):
        summed = self.mine[0].astype(f32)
        for d in (1, 2, 3):
            self.third[d].wait_recv()
            summed += self.got3[d].astype(f32)
        here = (self.rows, self.part(self.spot))
        self.fin[here] = summed.astype(bf16)
        self.fourth = []
        for e in (1, 2, 3):
            self.fourth.append(
                self.go(self.fin.at[here], self.fin.at[here], self.s4.at[e], self.r4.at[e], self.plane[e - 1])
            )

    def cross(self):
        for copy in self.fourth:
            copy.wait_recv()
        self.last = self.go(
            self.fin.at[self.rows], self.fin.at[self.rows], self.s5.at[0], self.r5.at[0], self.twin
        )

    def finish(self):
        self.last.wait_recv()
        for copy in self.sent:
            copy.wait_send()


def flow_scratch(depth, wide):
    dma = pltpu.SemaphoreType.DMA
    half, cols = depth // 2, wide // 4
    return [
        VMEM((4, half, wide), bf16),
        VMEM((4, half, wide), bf16),
        VMEM((4, 3, half, cols), bf16),
        VMEM((4, half, cols), bf16),
        VMEM((4, half, cols), bf16),
    ], [
        dma((4,)), dma((4,)), dma((12,)), dma((12,)), dma((4,)), dma((4,)),
        dma((4,)), dma((4,)), dma((1,)), dma((1,)),
    ]


def normed(x):
    average = jnp.mean(x, axis=-1, keepdims=True)
    centered = x - average
    inverse = lax.rsqrt(jnp.mean(centered * centered, axis=-1, keepdims=True) + norm_eps)
    return centered * inverse, inverse


def norm_back(grad, unit, inverse, gain):
    scaled = grad * gain
    return inverse * (
        scaled
        - jnp.mean(scaled, axis=-1, keepdims=True)
        - unit * jnp.mean(scaled * unit, axis=-1, keepdims=True)
    )


def total(x):
    return jnp.sum(x, axis=0, keepdims=True)


def key_present(shape, axis, span, padded, start, valid):
    slot = lax.broadcasted_iota(jnp.int32, shape, axis) + start
    owner = slot // padded
    inside = slot - owner * padded
    return (inside < span) & (owner * span + inside < valid)


def first_kernel(
    span, valid_ref, wh_in, wm_in, we_in, wr_in, x_ref, s_in, oc_ref,
    out_ref, ga_ref, g_ref, gm_ref, v_ref, mc_ref, st_ref, qkv_ref, dq_ref, wb_ref, s_ref,
    mixed_s, mc_s, prob_s, wr_s, x_all, wa_ref, xs, xr, ss, sr, *sems,
):
    fb = Fetch(wb_ref, *sems[:6])
    fa = Fetch(wa_ref, *sems[6:])
    over_z, plane, twin = team_devices()
    z = lax.axis_index("grp")
    valid = valid_ref[0]
    n, padded, width = x_all.shape
    depth = wb_ref.shape[1]
    hidden = 4 * width
    c1, c2 = 3 * width, 4 * width
    wb_ref[z, :, :c1] = wh_in[...]
    wb_ref[z, :, c1:] = wm_in[...]
    wa_ref[z, :, :c2] = we_in[...]
    for j in range(4):
        wa_ref[z, :, c2 + j * width : c2 + (j + 1) * width] = wr_in[j * depth : (j + 1) * depth, :]
    greet(over_z + plane + [twin])
    fb.to_group()
    others = []
    for d in (1, 2, 3):
        p = remote(s_in, s_ref.at[z], ss.at[d], sr.at[d], over_z[d - 1])
        q = remote(x_ref, x_all.at[z], xs.at[d], xr.at[d], over_z[d - 1])
        p.start()
        q.start()
        others += [p, q]
    fa.to_group()
    x_all[z] = x_ref[...]
    s_ref[z] = s_in[...]
    fb.to_plane()
    for copy in others:
        copy.wait()
    fa.to_plane()
    fb.to_twin()
    vec = s_ref[0].astype(f32) + s_ref[1].astype(f32) + s_ref[2].astype(f32) + s_ref[3].astype(f32)
    gain1, bias1, mixb, gain2, bias2, redb = [vec[i : i + 1] for i in range(6)]
    hb_q, hb_v = vec[6:7], vec[7:8]
    expb = jnp.concatenate([vec[8:9], vec[9:10], vec[10:11], vec[11:12]], 1)
    unit, _ = normed(x_all[...].reshape(n * padded, width).astype(f32))
    low = (unit * gain1 + bias1).astype(bf16)
    fb.arrive()
    w_heads = wb_ref[:, :, :c1].reshape(width, c1)
    proj = dot_nn(low, w_heads)
    qkv_ref[:, :width] = (proj[:, :width] + hb_q).astype(bf16)
    qkv_ref[:, width : 2 * width] = proj[:, width : 2 * width].astype(bf16)
    qkv_ref[:, 2 * width :] = (proj[:, 2 * width :] + hb_v).astype(bf16)
    own = pl.ds(pl.multiple_of(z * padded, 16), padded)
    scale = HEAD_DIM ** (-0.5)
    present = key_present((padded, n * padded), 1, span, padded, 0, valid)
    lses = []
    for head in range(HEADS):
        lo = head * HEAD_DIM
        q = qkv_ref[own, lo : lo + HEAD_DIM]
        k = qkv_ref[:, width + lo : width + lo + HEAD_DIM]
        v = qkv_ref[:, 2 * width + lo : 2 * width + lo + HEAD_DIM]
        scores = jnp.where(present, dot_nt(q, k) * scale, masked_score)
        top = jnp.max(scores, axis=-1, keepdims=True)
        e = jnp.exp(scores - top)
        row = jnp.sum(e, axis=-1, keepdims=True)
        prob = e / row
        prob_s[head] = prob
        lses.append(top + jnp.log(row))
        mixed_s[:, lo : lo + HEAD_DIM] = dot_nn(prob.astype(bf16), v).astype(bf16)
    fa.to_twin()
    w_mix = wb_ref[:, :, c1:].reshape(width, width)
    mixed = mixed_s[...]
    after = x_ref[...].astype(f32) + dot_nn(mixed, w_mix) + mixb
    unit2, inv2 = normed(after)
    low2 = (unit2 * gain2 + bias2).astype(bf16)
    fa.arrive()
    w_exp = wa_ref[:, :, :c2].reshape(width, hidden)
    pre = dot_nn(low2, w_exp) + expb
    cube = 0.044715
    root = 0.7978845608028654
    t = jnp.tanh(root * (pre + cube * (pre * pre * pre)))
    act = (0.5 * pre * (1.0 + t)).astype(bf16)
    slope = 0.5 * (1.0 + t) + (0.5 * root) * pre * (1.0 - t * t) * (1.0 + (3.0 * cube) * pre * pre)
    for i in range(n):
        for j in range(4):
            lo = i * width + j * depth
            wr_s[lo : lo + depth, :] = wa_ref[i, :, c2 + j * width : c2 + (j + 1) * width]
    w_red = wr_s[...]
    out_ref[...] = (after + dot_nn(act, w_red) + redb).astype(bf16)

    oc = oc_ref[...]
    ocf = oc.astype(f32)
    v_ref[...] = jnp.zeros(v_ref.shape, f32)
    v_ref[5:6, :] = total(ocf)
    g_red = dot_tn(act, oc).astype(bf16)
    for i in range(n):
        for j in range(4):
            lo = i * width + j * depth
            g_ref[i, :, c2 + j * width : c2 + (j + 1) * width] = g_red[lo : lo + depth]
    pre_cot = (slope * dot_nt(oc, w_red)).astype(bf16)
    pre_sum = total(pre_cot.astype(f32))
    for i in range(4):
        v_ref[8 + i : 9 + i, :] = pre_sum[:, i * width : (i + 1) * width]
    g_ref[:, :, :c2] = dot_tn(low2, pre_cot).astype(bf16).reshape(n, depth, hidden)
    grad2 = dot_nt(pre_cot, w_exp)
    v_ref[3:4, :] = total(grad2 * unit2)
    v_ref[4:5, :] = total(grad2)
    grad_after = ocf + norm_back(grad2, unit2, inv2, gain2)
    ga_ref[...] = grad_after
    attn_cot = grad_after.astype(bf16)
    v_ref[2:3, :] = total(attn_cot.astype(f32))
    gm_ref[...] = dot_tn(mixed, attn_cot).astype(bf16).reshape(n, depth, width)
    mc_s[...] = dot_nt(attn_cot, w_mix).astype(bf16)
    mc_ref[...] = mc_s[...]
    cols = []
    for head in range(HEADS):
        lo = head * HEAD_DIM
        k = qkv_ref[:, width + lo : width + lo + HEAD_DIM]
        v = qkv_ref[:, 2 * width + lo : 2 * width + lo + HEAD_DIM]
        prob = prob_s[head]
        grad_prob = dot_nt(mc_s[:, lo : lo + HEAD_DIM], v)
        inner = jnp.sum(prob * grad_prob, axis=-1, keepdims=True)
        cols.append(inner)
        score_cot = (prob * (grad_prob - inner)).astype(bf16)
        dq_ref[:, lo : lo + HEAD_DIM] = (dot_nn(score_cot, k) * scale).astype(bf16)
    lane = lax.broadcasted_iota(jnp.int32, (padded, 128), 1)
    stats = jnp.zeros((padded, 128), f32)
    for head in range(HEADS):
        stats = jnp.where(lane == head, lses[head], stats)
        stats = jnp.where(lane == head + 8, cols[head], stats)
    st_ref[...] = stats.T[:ROWS, :]
    fb.finish()
    fa.finish()


def first_call(span, valid, weights, x, s, oc):
    n = 4
    padded, width = x.shape
    depth = weights[1].shape[0]
    dma = pltpu.SemaphoreType.DMA
    fetch = [dma((4,)), dma((4,)), dma((9,)), dma((9,)), dma((4,)), dma((4,))]
    shape = jax.ShapeDtypeStruct
    vmem = pl.BlockSpec(memory_space=VMEM)
    return pl.pallas_call(
        functools.partial(first_kernel, span),
        out_shape=[
            shape((padded, width), bf16),
            shape((padded, width), f32),
            shape((n, depth, 8 * width), bf16),
            shape((n, depth, width), bf16),
            shape((ROWS, width), f32),
            shape((padded, width), bf16),
            shape((ROWS, padded), f32),
            shape((n * padded, 3 * width), bf16),
            shape((padded, width), bf16),
            shape((n, depth, 4 * width), bf16),
            shape((n,) + s.shape, bf16),
        ],
        in_specs=[pl.BlockSpec(memory_space=pltpu.SMEM)] + [vmem] * 7,
        out_specs=[vmem] * 11,
        scratch_shapes=[
            VMEM((padded, width), bf16),
            VMEM((padded, width), bf16),
            VMEM((HEADS, padded, n * padded), f32),
            VMEM((4 * width, width), bf16),
            VMEM((n, padded, width), bf16),
            VMEM((n, depth, 8 * width), bf16),
            dma((4,)), dma((4,)), dma((4,)), dma((4,)),
        ] + fetch + fetch,
        compiler_params=pltpu.CompilerParams(
            collective_id=0, has_side_effects=True, vmem_limit_bytes=LIMIT
        ),
        name="gather_forward_and_feed_back",
    )(valid, *weights, x, s, oc)


def second_kernel(
    span, valid_ref, w_ref, s_ref, x_ref, ga_ref, mc_in, st_in, qkv_ref, dq_ref, g_in, gm_ref, v_in,
    ig_ref, fa_ref, fb_ref, ov_ref, *scratch,
):
    hc_s, mc_ref, st_ref, gb, v_ref, v1, va, v2, vb, v3, ms, mr, ts, tr, sv, rv = scratch[:16]
    fa = Flow(g_in, *scratch[16:21], fa_ref, *scratch[21:31])
    fb = Flow(gb, *scratch[31:36], fb_ref, *scratch[36:46])
    z = lax.axis_index("grp")
    over_z, plane, twin = team_devices()
    valid = valid_ref[0]
    padded, width = x_ref.shape
    n = mc_ref.shape[0]
    depth = w_ref.shape[1]
    greet(over_z + plane + [twin])
    cots = []
    for d in (1, 2, 3):
        a = remote(mc_in, mc_ref.at[z], ms.at[d], mr.at[d], over_z[d - 1])
        b = remote(st_in, st_ref.at[z], ts.at[d], tr.at[d], over_z[d - 1])
        a.start()
        b.start()
        cots += [a, b]
    fa.to_twin()
    mc_ref[z] = mc_in[...]
    st_ref[z] = st_in[...]
    hc_s[:, :width] = dq_ref[...]
    gb[:, :, 3 * width :] = gm_ref[...]
    vec = s_ref[0].astype(f32) + s_ref[1].astype(f32) + s_ref[2].astype(f32) + s_ref[3].astype(f32)
    gain1, bias1 = vec[0:1], vec[1:2]
    fa.to_plane()
    for copy in cots:
        copy.wait()
    own = pl.ds(pl.multiple_of(z * padded, 16), padded)
    scale = HEAD_DIM ** (-0.5)
    present = key_present((padded, n * padded), 0, span, padded, z * padded, valid)
    for head in range(HEADS):
        lo = head * HEAD_DIM
        q = qkv_ref[:, lo : lo + HEAD_DIM]
        k = qkv_ref[own, width + lo : width + lo + HEAD_DIM]
        v = qkv_ref[own, 2 * width + lo : 2 * width + lo + HEAD_DIM]
        mc = mc_ref[:, :, lo : lo + HEAD_DIM].reshape(n * padded, HEAD_DIM)
        lse = jnp.concatenate([st_ref[i, head : head + 1, :] for i in range(n)], 1)
        inner = jnp.concatenate([st_ref[i, head + 8 : head + 9, :] for i in range(n)], 1)
        prob = jnp.exp(jnp.where(present, dot_nt(k, q) * scale, masked_score) - lse)
        grad_prob = dot_nt(v, mc)
        hc_s[:, 2 * width + lo : 2 * width + lo + HEAD_DIM] = dot_nn(prob.astype(bf16), mc).astype(bf16)
        score_cot = (prob * (grad_prob - inner)).astype(bf16)
        hc_s[:, width + lo : width + lo + HEAD_DIM] = (dot_nn(score_cot, q) * scale).astype(bf16)
    unit, inverse = normed(x_ref[...].astype(f32))
    low = (unit * gain1 + bias1).astype(bf16)
    hc = hc_s[...]
    gb[:, :, : 3 * width] = dot_tn(low, hc).astype(bf16).reshape(n, depth, 3 * width)
    fb.to_twin()
    v_ref[...] = v_in[...]
    v_ref[6:7, :] = total(hc[:, :width].astype(f32))
    v_ref[7:8, :] = total(hc[:, 2 * width :].astype(f32))
    grad = dot_nt(hc, w_ref[:, :, : 3 * width].reshape(width, 3 * width))
    v_ref[0:1, :] = total(grad * unit)
    v_ref[1:2, :] = total(grad)
    vecs = [remote(v_ref, v1, sv.at[0], rv.at[0], twin)]
    vecs[0].start()
    fb.to_plane()
    fa.to_group()
    ig_ref[...] = ga_ref[...] + norm_back(grad, unit, inverse, gain1)
    vecs[0].wait_recv()
    va[...] = v_ref[...] + v1[...]
    for e in (1, 2, 3):
        copy = remote(va, v2.at[e - 1], sv.at[e], rv.at[e], plane[e - 1])
        copy.start()
        vecs.append(copy)
    fb.to_group()
    for e in (1, 2, 3):
        vecs[e].wait_recv()
    vb[...] = va[...] + v2[0] + v2[1] + v2[2]
    for d in (1, 2, 3):
        copy = remote(vb, v3.at[d - 1], sv.at[d + 3], rv.at[d + 3], over_z[d - 1])
        copy.start()
        vecs.append(copy)
    fa.spread()
    fb.spread()
    fa.cross()
    fb.cross()
    for d in (4, 5, 6):
        vecs[d].wait_recv()
    ov_ref[...] = vb[...] + v3[0] + v3[1] + v3[2]
    fa.finish()
    fb.finish()
    for copy in vecs:
        copy.wait_send()


def second_call(span, valid, w, s, x, ga, mc, st, qkv, dq, g, gm, v):
    padded, width = x.shape
    depth = w.shape[1]
    shape = jax.ShapeDtypeStruct
    vmem = pl.BlockSpec(memory_space=VMEM)
    dma = pltpu.SemaphoreType.DMA
    bufs_a, sems_a = flow_scratch(depth, 8 * width)
    bufs_b, sems_b = flow_scratch(depth, 4 * width)
    return pl.pallas_call(
        functools.partial(second_kernel, span),
        out_shape=[
            shape((padded, width), f32), shape((depth, 8 * width), bf16),
            shape((depth, 4 * width), bf16), shape(v.shape, f32),
        ],
        in_specs=[pl.BlockSpec(memory_space=pltpu.SMEM)] + [vmem] * 11,
        out_specs=[vmem] * 4,
        scratch_shapes=[
            VMEM((padded, 3 * width), bf16),
            VMEM((4,) + mc.shape, bf16),
            VMEM((4,) + st.shape, f32),
            VMEM((4, depth, 4 * width), bf16),
            VMEM(v.shape, f32),
            VMEM(v.shape, f32),
            VMEM(v.shape, f32),
            VMEM((3,) + v.shape, f32),
            VMEM(v.shape, f32),
            VMEM((3,) + v.shape, f32),
            dma((4,)), dma((4,)), dma((4,)), dma((4,)), dma((7,)), dma((7,)),
        ] + bufs_a + sems_a + bufs_b + sems_b,
        compiler_params=pltpu.CompilerParams(
            collective_id=1, has_side_effects=True, vmem_limit_bytes=LIMIT
        ),
        name="attention_back_and_sum",
    )(valid, w, s, x, ga, mc, st, qkv, dq, g, gm, v)


def unpack_kernel(a_ref, b_ref, h_ref, m_ref, e_ref, r_ref):
    depth, width = m_ref.shape
    h_ref[...] = b_ref[:, : 3 * width].astype(f32)
    m_ref[...] = b_ref[:, 3 * width :].astype(f32)
    e_ref[...] = a_ref[:, : 4 * width].astype(f32)
    for j in range(4):
        lo = (4 + j) * width
        r_ref[j * depth : (j + 1) * depth, :] = a_ref[:, lo : lo + width].astype(f32)


def unpack_call(a, b):
    depth, width = a.shape[0], a.shape[1] // 8
    shape = jax.ShapeDtypeStruct
    vmem = pl.BlockSpec(memory_space=VMEM)
    return pl.pallas_call(
        unpack_kernel,
        out_shape=[
            shape((depth, 3 * width), f32), shape((depth, width), f32),
            shape((depth, 4 * width), f32), shape((4 * depth, width), f32),
        ],
        in_specs=[vmem] * 2,
        out_specs=[vmem] * 4,
        compiler_params=pltpu.CompilerParams(vmem_limit_bytes=LIMIT),
        name="unpack",
    )(a, b)


def on_device(
    image_tokens, valid_count, first_gain, first_bias, heads_weight, heads_bias,
    mixing_weight, mixing_bias, second_gain, second_bias, expand_weight, expand_bias,
    reduce_weight, reduce_bias, output_cotangent,
):
    _, span, width = image_tokens.shape
    depth = heads_weight.shape[0]
    padded = up(span, 16)
    z = lax.axis_index("grp")

    def pad_rows(x):
        return jnp.pad(x[0], ((0, padded - span), (0, 0)))

    x = pad_rows(image_tokens)
    oc = pad_rows(output_cotangent)
    ones = jnp.stack([first_gain, first_bias, mixing_bias, second_gain, second_bias, reduce_bias])
    col = jnp.arange(width) // depth == z
    rows6 = jnp.where(col[None, :], jnp.tile(ones, (1, 4)), 0)
    twos = jnp.where(jnp.arange(2 * width) // (2 * depth) == z, jnp.tile(heads_bias, 4), 0)
    fours = jnp.where(jnp.arange(4)[:, None] == z, expand_bias[None, :], 0)
    s = jnp.concatenate(
        [rows6, twos.reshape(2, width), fours, jnp.zeros((ROWS - 12, width), bf16)], 0
    ).astype(bf16)

    weights = (heads_weight, mixing_weight, expand_weight, reduce_weight)
    out, ga, g, gm, v, mc, st, qkv, dq, w_all, s_all = first_call(
        span, valid_count, weights, x, s, oc
    )
    ig, ga_sum, gb_sum, v = second_call(
        span, valid_count, w_all, s_all, x, ga, mc, st, qkv, dq, g, gm, v
    )
    teams = lax.axis_size("rep") // TEAM
    if teams > 1:
        ga_sum, gb_sum, v = lax.psum(
            (ga_sum.astype(f32) / TEAM, gb_sum.astype(f32) / TEAM, v / TEAM), "rep"
        )
    g_heads, g_mix, g_exp, g_red = unpack_call(ga_sum, gb_sum)
    six = lax.dynamic_slice(v, (0, z * depth), (6, depth))
    two = lax.dynamic_slice(v[6:8].reshape(2 * width), (z * 2 * depth,), (2 * depth,))
    four = lax.dynamic_slice(v, (8 + z, 0), (1, width))[0]
    return (
        out[None, :span], ig[None, :span],
        six[0], six[1], g_heads, two, g_mix, six[2], six[3], six[4],
        g_exp, four, g_red, six[5],
    )


def solution(mesh):
    tokens = P("rep", "grp", None)
    vec, mat = P("grp"), P("grp", None)
    weights = (vec, vec, mat, vec, mat, vec, vec, vec, mat, vec, mat, vec)
    return jax.shard_map(
        on_device,
        mesh=mesh,
        in_specs=(tokens, P("rep")) + weights + (tokens,),
        out_specs=(tokens, tokens) + weights,
        check_vma=False,
    )
```

```python
import functools

import jax
import jax.numpy as jnp
from jax import lax
from jax.experimental import pallas as pl
from jax.experimental.pallas import tpu as pltpu
from jax.sharding import PartitionSpec as P

HEADS = 6
HEAD_DIM = 64
ROWS = 16
TEAM = 8

norm_eps = 1e-06
masked_score = -1000000000.0
f32 = jnp.float32
bf16 = jnp.bfloat16
MESH = pl.DeviceIdType.MESH
VMEM = pltpu.VMEM
LIMIT = 56 * 1024 * 1024


def up(count, unit):
    return (count + unit - 1) // unit * unit


def dot_nn(a, b):
    return lax.dot_general(a, b, (((1,), (0,)), ((), ())), preferred_element_type=f32)


def dot_nt(a, b):
    return lax.dot_general(a, b, (((1,), (1,)), ((), ())), preferred_element_type=f32)


def dot_tn(a, b):
    return lax.dot_general(a, b, (((0,), (0,)), ((), ())), preferred_element_type=f32)


def places():
    rep = lax.axis_index("rep")
    z = lax.axis_index("grp")
    core = lax.rem(rep, 2)
    spot = lax.rem(rep // 2, 4)
    base = rep - lax.rem(rep, TEAM)
    return rep, z, core, spot, base


def greet(devices):
    barrier = pltpu.get_barrier_semaphore()
    for device in devices:
        pl.semaphore_signal(barrier, inc=1, device_id=device, device_id_type=MESH)
    pl.semaphore_wait(barrier, len(devices))


def remote(src, dst, send, recv, device):
    copy = pltpu.make_async_remote_copy(
        src_ref=src, dst_ref=dst, send_sem=send, recv_sem=recv,
        device_id=device, device_id_type=MESH,
    )
    return copy


def team_devices():
    rep, z, core, spot, base = places()
    over_z = [(rep, lax.rem(z + d, 4)) for d in (1, 2, 3)]
    plane = [(base + lax.rem(spot + e, 4) * 2 + core, z) for e in (1, 2, 3)]
    twin = (base + spot * 2 + 1 - core, z)
    return over_z, plane, twin


class Fetch:
    def __init__(self, w, zs, zr, ps, pr, cs, cr):
        self.__dict__.update(locals())
        rep, self.z, core, spot, base = places()
        self.over_z, self.plane, self.twin = team_devices()
        half, cols = w.shape[1] // 2, w.shape[2] // 4
        self.rows = pl.ds(pl.multiple_of(core * half, 16), half)
        self.part = pl.ds(pl.multiple_of(spot * cols, 128), cols)
        self.sent = []

    def go(self, here, *args):
        copy = remote(here, here, *args)
        copy.start()
        self.sent.append(copy)
        return copy

    def to_group(self):
        self.first = {}
        for d in (1, 2, 3):
            here = self.w.at[self.z, self.rows, self.part]
            self.first[d] = self.go(here, self.zs.at[d], self.zr.at[d], self.over_z[d - 1])

    def to_plane(self):
        self.second = {}
        for d in (1, 2, 3):
            owner = lax.rem(self.z + 4 - d, 4)
            self.first[d].wait_recv()
            for e in (1, 2, 3):
                here = self.w.at[owner, self.rows, self.part]
                k = d * 3 + e - 4
                self.second[d, e] = self.go(here, self.ps.at[k], self.pr.at[k], self.plane[e - 1])

    def to_twin(self):
        self.third = []
        for d in (1, 2, 3):
            owner = lax.rem(self.z + 4 - d, 4)
            for e in (1, 2, 3):
                self.second[d, e].wait_recv()
            here = self.w.at[owner, self.rows]
            self.third.append(self.go(here, self.cs.at[d], self.cr.at[d], self.twin))

    def arrive(self):
        for copy in self.third:
            copy.wait_recv()

    def finish(self):
        for copy in self.sent:
            copy.wait_send()


class Flow:
    def __init__(self, g, got1, h, got2, mine, got3, fin, s1, r1, s2, r2, s3, r3, s4, r4, s5, r5):
        self.__dict__.update(locals())
        rep, self.z, self.core, self.spot, base = places()
        self.over_z, self.plane, self.twin = team_devices()
        half = g.shape[1] // 2
        self.cols = g.shape[2] // 4
        self.rows = pl.ds(pl.multiple_of(self.core * half, 16), half)
        self.away = pl.ds(pl.multiple_of((1 - self.core) * half, 16), half)
        self.order = (2, 1, 3, 0)
        self.sent = []

    def part(self, index):
        return pl.ds(pl.multiple_of(index * self.cols, 128), self.cols)

    def go(self, *args):
        copy = remote(*args)
        copy.start()
        self.sent.append(copy)
        return copy

    def to_twin(self):
        self.first = {}
        for d in self.order:
            to = lax.rem(self.z + d, 4)
            self.first[d] = self.go(
                self.g.at[to, self.away], self.got1.at[d], self.s1.at[d], self.r1.at[d], self.twin
            )

    def to_plane(self):
        self.second = {}
        for d in self.order:
            to = lax.rem(self.z + d, 4)
            self.first[d].wait_recv()
            both = self.g[to, self.rows, :].astype(f32) + self.got1[d].astype(f32)
            self.h[d] = both.astype(bf16)
            for e in (1, 2, 3):
                there = lax.rem(self.spot + e, 4)
                k = d * 3 + e - 1
                self.second[d, e] = self.go(
                    self.h.at[d, :, self.part(there)], self.got2.at[d, e - 1],
                    self.s2.at[k], self.r2.at[k], self.plane[e - 1],
                )

    def to_group(self):
        self.third = {}
        for d in self.order:
            summed = self.h[d, :, self.part(self.spot)].astype(f32)
            for e in (1, 2, 3):
                self.second[d, e].wait_recv()
                summed += self.got2[d, e - 1].astype(f32)
            self.mine[d] = summed.astype(bf16)
            if d:
                self.third[d] = self.go(
                    self.mine.at[d], self.got3.at[d], self.s3.at[d], self.r3.at[d], self.over_z[d - 1]
                )

    def spread(self):
        summed = self.mine[0].astype(f32)
        for d in (1, 2, 3):
            self.third[d].wait_recv()
            summed += self.got3[d].astype(f32)
        here = (self.rows, self.part(self.spot))
        self.fin[here] = summed.astype(bf16)
        self.fourth = []
        for e in (1, 2, 3):
            self.fourth.append(
                self.go(self.fin.at[here], self.fin.at[here], self.s4.at[e], self.r4.at[e], self.plane[e - 1])
            )

    def cross(self):
        for copy in self.fourth:
            copy.wait_recv()
        self.last = self.go(
            self.fin.at[self.rows], self.fin.at[self.rows], self.s5.at[0], self.r5.at[0], self.twin
        )

    def finish(self):
        self.last.wait_recv()
        for copy in self.sent:
            copy.wait_send()


def flow_scratch(depth, wide):
    dma = pltpu.SemaphoreType.DMA
    half, cols = depth // 2, wide // 4
    return [
        VMEM((4, half, wide), bf16),
        VMEM((4, half, wide), bf16),
        VMEM((4, 3, half, cols), bf16),
        VMEM((4, half, cols), bf16),
        VMEM((4, half, cols), bf16),
    ], [
        dma((4,)), dma((4,)), dma((12,)), dma((12,)), dma((4,)), dma((4,)),
        dma((4,)), dma((4,)), dma((1,)), dma((1,)),
    ]


def normed(x):
    average = jnp.mean(x, axis=-1, keepdims=True)
    centered = x - average
    inverse = lax.rsqrt(jnp.mean(centered * centered, axis=-1, keepdims=True) + norm_eps)
    return centered * inverse, inverse


def norm_back(grad, unit, inverse, gain):
    scaled = grad * gain
    return inverse * (
        scaled
        - jnp.mean(scaled, axis=-1, keepdims=True)
        - unit * jnp.mean(scaled * unit, axis=-1, keepdims=True)
    )


def total(x):
    return jnp.sum(x, axis=0, keepdims=True)


def key_present(shape, axis, span, padded, start, valid):
    slot = lax.broadcasted_iota(jnp.int32, shape, axis) + start
    owner = slot // padded
    inside = slot - owner * padded
    return (inside < span) & (owner * span + inside < valid)


def first_kernel(
    span, valid_ref, wh_in, wm_in, we_in, wr_in, x_ref, s_in, oc_ref,
    out_ref, ga_ref, g_ref, gm_ref, v_ref, mc_ref, st_ref, qkv_ref, dq_ref, wb_ref, s_ref,
    mixed_s, mc_s, prob_s, wr_s, x_all, wa_ref, xs, xr, ss, sr, *sems,
):
    fb = Fetch(wb_ref, *sems[:6])
    fa = Fetch(wa_ref, *sems[6:])
    over_z, plane, twin = team_devices()
    z = lax.axis_index("grp")
    valid = valid_ref[0]
    n, padded, width = x_all.shape
    depth = wb_ref.shape[1]
    hidden = 4 * width
    c1, c2 = 3 * width, 4 * width
    wb_ref[z, :, :c1] = wh_in[...]
    wb_ref[z, :, c1:] = wm_in[...]
    wa_ref[z, :, :c2] = we_in[...]
    for j in range(4):
        wa_ref[z, :, c2 + j * width : c2 + (j + 1) * width] = wr_in[j * depth : (j + 1) * depth, :]
    greet(over_z + plane + [twin])
    fb.to_group()
    fa.to_group()
    others = []
    for d in (1, 2, 3):
        p = remote(s_in, s_ref.at[z], ss.at[d], sr.at[d], over_z[d - 1])
        q = remote(x_ref, x_all.at[z], xs.at[d], xr.at[d], over_z[d - 1])
        p.start()
        q.start()
        others += [p, q]
    x_all[z] = x_ref[...]
    s_ref[z] = s_in[...]
    fb.to_plane()
    fa.to_plane()
    fb.to_twin()
    for copy in others:
        copy.wait()
    vec = s_ref[0].astype(f32) + s_ref[1].astype(f32) + s_ref[2].astype(f32) + s_ref[3].astype(f32)
    gain1, bias1, mixb, gain2, bias2, redb = [vec[i : i + 1] for i in range(6)]
    hb_q, hb_v = vec[6:7], vec[7:8]
    expb = jnp.concatenate([vec[8:9], vec[9:10], vec[10:11], vec[11:12]], 1)
    unit, _ = normed(x_all[...].reshape(n * padded, width).astype(f32))
    low = (unit * gain1 + bias1).astype(bf16)
    fb.arrive()
    w_heads = wb_ref[:, :, :c1].reshape(width, c1)
    proj = dot_nn(low, w_heads)
    qkv_ref[:, :width] = (proj[:, :width] + hb_q).astype(bf16)
    qkv_ref[:, width : 2 * width] = proj[:, width : 2 * width].astype(bf16)
    qkv_ref[:, 2 * width :] = (proj[:, 2 * width :] + hb_v).astype(bf16)
    own = pl.ds(pl.multiple_of(z * padded, 16), padded)
    scale = HEAD_DIM ** (-0.5)
    present = key_present((padded, n * padded), 1, span, padded, 0, valid)
    lses = []
    for head in range(HEADS):
        lo = head * HEAD_DIM
        q = qkv_ref[own, lo : lo + HEAD_DIM]
        k = qkv_ref[:, width + lo : width + lo + HEAD_DIM]
        v = qkv_ref[:, 2 * width + lo : 2 * width + lo + HEAD_DIM]
        scores = jnp.where(present, dot_nt(q, k) * scale, masked_score)
        top = jnp.max(scores, axis=-1, keepdims=True)
        e = jnp.exp(scores - top)
        row = jnp.sum(e, axis=-1, keepdims=True)
        prob = e / row
        prob_s[head] = prob
        lses.append(top + jnp.log(row))
        mixed_s[:, lo : lo + HEAD_DIM] = dot_nn(prob.astype(bf16), v).astype(bf16)
    fa.to_twin()
    w_mix = wb_ref[:, :, c1:].reshape(width, width)
    mixed = mixed_s[...]
    after = x_ref[...].astype(f32) + dot_nn(mixed, w_mix) + mixb
    unit2, inv2 = normed(after)
    low2 = (unit2 * gain2 + bias2).astype(bf16)
    fa.arrive()
    w_exp = wa_ref[:, :, :c2].reshape(width, hidden)
    pre = dot_nn(low2, w_exp) + expb
    cube = 0.044715
    root = 0.7978845608028654
    t = jnp.tanh(root * (pre + cube * (pre * pre * pre)))
    act = (0.5 * pre * (1.0 + t)).astype(bf16)
    slope = 0.5 * (1.0 + t) + (0.5 * root) * pre * (1.0 - t * t) * (1.0 + (3.0 * cube) * pre * pre)
    for i in range(n):
        for j in range(4):
            lo = i * width + j * depth
            wr_s[lo : lo + depth, :] = wa_ref[i, :, c2 + j * width : c2 + (j + 1) * width]
    w_red = wr_s[...]
    out_ref[...] = (after + dot_nn(act, w_red) + redb).astype(bf16)

    oc = oc_ref[...]
    ocf = oc.astype(f32)
    v_ref[...] = jnp.zeros(v_ref.shape, f32)
    v_ref[5:6, :] = total(ocf)
    g_red = dot_tn(act, oc).astype(bf16)
    for i in range(n):
        for j in range(4):
            lo = i * width + j * depth
            g_ref[i, :, c2 + j * width : c2 + (j + 1) * width] = g_red[lo : lo + depth]
    pre_cot = (slope * dot_nt(oc, w_red)).astype(bf16)
    pre_sum = total(pre_cot.astype(f32))
    for i in range(4):
        v_ref[8 + i : 9 + i, :] = pre_sum[:, i * width : (i + 1) * width]
    g_ref[:, :, :c2] = dot_tn(low2, pre_cot).astype(bf16).reshape(n, depth, hidden)
    grad2 = dot_nt(pre_cot, w_exp)
    v_ref[3:4, :] = total(grad2 * unit2)
    v_ref[4:5, :] = total(grad2)
    grad_after = ocf + norm_back(grad2, unit2, inv2, gain2)
    ga_ref[...] = grad_after
    attn_cot = grad_after.astype(bf16)
    v_ref[2:3, :] = total(attn_cot.astype(f32))
    gm_ref[...] = dot_tn(mixed, attn_cot).astype(bf16).reshape(n, depth, width)
    mc_s[...] = dot_nt(attn_cot, w_mix).astype(bf16)
    mc_ref[...] = mc_s[...]
    cols = []
    for head in range(HEADS):
        lo = head * HEAD_DIM
        k = qkv_ref[:, width + lo : width + lo + HEAD_DIM]
        v = qkv_ref[:, 2 * width + lo : 2 * width + lo + HEAD_DIM]
        prob = prob_s[head]
        grad_prob = dot_nt(mc_s[:, lo : lo + HEAD_DIM], v)
        inner = jnp.sum(prob * grad_prob, axis=-1, keepdims=True)
        cols.append(inner)
        score_cot = (prob * (grad_prob - inner)).astype(bf16)
        dq_ref[:, lo : lo + HEAD_DIM] = (dot_nn(score_cot, k) * scale).astype(bf16)
    lane = lax.broadcasted_iota(jnp.int32, (padded, 128), 1)
    stats = jnp.zeros((padded, 128), f32)
    for head in range(HEADS):
        stats = jnp.where(lane == head, lses[head], stats)
        stats = jnp.where(lane == head + 8, cols[head], stats)
    st_ref[...] = stats.T[:ROWS, :]
    fb.finish()
    fa.finish()


def first_call(span, valid, weights, x, s, oc):
    n = 4
    padded, width = x.shape
    depth = weights[1].shape[0]
    dma = pltpu.SemaphoreType.DMA
    fetch = [dma((4,)), dma((4,)), dma((9,)), dma((9,)), dma((4,)), dma((4,))]
    shape = jax.ShapeDtypeStruct
    vmem = pl.BlockSpec(memory_space=VMEM)
    return pl.pallas_call(
        functools.partial(first_kernel, span),
        out_shape=[
            shape((padded, width), bf16),
            shape((padded, width), f32),
            shape((n, depth, 8 * width), bf16),
            shape((n, depth, width), bf16),
            shape((ROWS, width), f32),
            shape((padded, width), bf16),
            shape((ROWS, padded), f32),
            shape((n * padded, 3 * width), bf16),
            shape((padded, width), bf16),
            shape((n, depth, 4 * width), bf16),
            shape((n,) + s.shape, bf16),
        ],
        in_specs=[pl.BlockSpec(memory_space=pltpu.SMEM)] + [vmem] * 7,
        out_specs=[vmem] * 11,
        scratch_shapes=[
            VMEM((padded, width), bf16),
            VMEM((padded, width), bf16),
            VMEM((HEADS, padded, n * padded), f32),
            VMEM((4 * width, width), bf16),
            VMEM((n, padded, width), bf16),
            VMEM((n, depth, 8 * width), bf16),
            dma((4,)), dma((4,)), dma((4,)), dma((4,)),
        ] + fetch + fetch,
        compiler_params=pltpu.CompilerParams(
            collective_id=0, has_side_effects=True, vmem_limit_bytes=LIMIT
        ),
        name="gather_forward_and_feed_back",
    )(valid, *weights, x, s, oc)


def second_kernel(
    span, valid_ref, w_ref, s_ref, x_ref, ga_ref, mc_in, st_in, qkv_ref, dq_ref, g_in, gm_ref, v_in,
    ig_ref, fa_ref, fb_ref, ov_ref, *scratch,
):
    hc_s, mc_ref, st_ref, gb, v_ref, v1, va, v2, vb, v3, ms, mr, ts, tr, sv, rv = scratch[:16]
    fa = Flow(g_in, *scratch[16:21], fa_ref, *scratch[21:31])
    fb = Flow(gb, *scratch[31:36], fb_ref, *scratch[36:46])
    z = lax.axis_index("grp")
    over_z, plane, twin = team_devices()
    valid = valid_ref[0]
    padded, width = x_ref.shape
    n = mc_ref.shape[0]
    depth = w_ref.shape[1]
    greet(over_z + plane + [twin])
    cots = []
    for d in (1, 2, 3):
        a = remote(mc_in, mc_ref.at[z], ms.at[d], mr.at[d], over_z[d - 1])
        b = remote(st_in, st_ref.at[z], ts.at[d], tr.at[d], over_z[d - 1])
        a.start()
        b.start()
        cots += [a, b]
    fa.to_twin()
    mc_ref[z] = mc_in[...]
    st_ref[z] = st_in[...]
    hc_s[:, :width] = dq_ref[...]
    gb[:, :, 3 * width :] = gm_ref[...]
    vec = s_ref[0].astype(f32) + s_ref[1].astype(f32) + s_ref[2].astype(f32) + s_ref[3].astype(f32)
    gain1, bias1 = vec[0:1], vec[1:2]
    fa.to_plane()
    for copy in cots:
        copy.wait()
    own = pl.ds(pl.multiple_of(z * padded, 16), padded)
    scale = HEAD_DIM ** (-0.5)
    present = key_present((padded, n * padded), 0, span, padded, z * padded, valid)
    for head in range(HEADS):
        lo = head * HEAD_DIM
        q = qkv_ref[:, lo : lo + HEAD_DIM]
        k = qkv_ref[own, width + lo : width + lo + HEAD_DIM]
        v = qkv_ref[own, 2 * width + lo : 2 * width + lo + HEAD_DIM]
        mc = mc_ref[:, :, lo : lo + HEAD_DIM].reshape(n * padded, HEAD_DIM)
        lse = jnp.concatenate([st_ref[i, head : head + 1, :] for i in range(n)], 1)
        inner = jnp.concatenate([st_ref[i, head + 8 : head + 9, :] for i in range(n)], 1)
        prob = jnp.exp(jnp.where(present, dot_nt(k, q) * scale, masked_score) - lse)
        grad_prob = dot_nt(v, mc)
        hc_s[:, 2 * width + lo : 2 * width + lo + HEAD_DIM] = dot_nn(prob.astype(bf16), mc).astype(bf16)
        score_cot = (prob * (grad_prob - inner)).astype(bf16)
        hc_s[:, width + lo : width + lo + HEAD_DIM] = (dot_nn(score_cot, q) * scale).astype(bf16)
    unit, inverse = normed(x_ref[...].astype(f32))
    low = (unit * gain1 + bias1).astype(bf16)
    hc = hc_s[...]
    gb[:, :, : 3 * width] = dot_tn(low, hc).astype(bf16).reshape(n, depth, 3 * width)
    fb.to_twin()
    v_ref[...] = v_in[...]
    v_ref[6:7, :] = total(hc[:, :width].astype(f32))
    v_ref[7:8, :] = total(hc[:, 2 * width :].astype(f32))
    grad = dot_nt(hc, w_ref[:, :, : 3 * width].reshape(width, 3 * width))
    v_ref[0:1, :] = total(grad * unit)
    v_ref[1:2, :] = total(grad)
    vecs = [remote(v_ref, v1, sv.at[0], rv.at[0], twin)]
    vecs[0].start()
    fb.to_plane()
    fa.to_group()
    ig_ref[...] = ga_ref[...] + norm_back(grad, unit, inverse, gain1)
    vecs[0].wait_recv()
    va[...] = v_ref[...] + v1[...]
    for e in (1, 2, 3):
        copy = remote(va, v2.at[e - 1], sv.at[e], rv.at[e], plane[e - 1])
        copy.start()
        vecs.append(copy)
    fb.to_group()
    for e in (1, 2, 3):
        vecs[e].wait_recv()
    vb[...] = va[...] + v2[0] + v2[1] + v2[2]
    for d in (1, 2, 3):
        copy = remote(vb, v3.at[d - 1], sv.at[d + 3], rv.at[d + 3], over_z[d - 1])
        copy.start()
        vecs.append(copy)
    fa.spread()
    fb.spread()
    fa.cross()
    fb.cross()
    for d in (4, 5, 6):
        vecs[d].wait_recv()
    ov_ref[...] = vb[...] + v3[0] + v3[1] + v3[2]
    fa.finish()
    fb.finish()
    for copy in vecs:
        copy.wait_send()


def second_call(span, valid, w, s, x, ga, mc, st, qkv, dq, g, gm, v):
    padded, width = x.shape
    depth = w.shape[1]
    shape = jax.ShapeDtypeStruct
    vmem = pl.BlockSpec(memory_space=VMEM)
    dma = pltpu.SemaphoreType.DMA
    bufs_a, sems_a = flow_scratch(depth, 8 * width)
    bufs_b, sems_b = flow_scratch(depth, 4 * width)
    return pl.pallas_call(
        functools.partial(second_kernel, span),
        out_shape=[
            shape((padded, width), f32), shape((depth, 8 * width), bf16),
            shape((depth, 4 * width), bf16), shape(v.shape, f32),
        ],
        in_specs=[pl.BlockSpec(memory_space=pltpu.SMEM)] + [vmem] * 11,
        out_specs=[vmem] * 4,
        scratch_shapes=[
            VMEM((padded, 3 * width), bf16),
            VMEM((4,) + mc.shape, bf16),
            VMEM((4,) + st.shape, f32),
            VMEM((4, depth, 4 * width), bf16),
            VMEM(v.shape, f32),
            VMEM(v.shape, f32),
            VMEM(v.shape, f32),
            VMEM((3,) + v.shape, f32),
            VMEM(v.shape, f32),
            VMEM((3,) + v.shape, f32),
            dma((4,)), dma((4,)), dma((4,)), dma((4,)), dma((7,)), dma((7,)),
        ] + bufs_a + sems_a + bufs_b + sems_b,
        compiler_params=pltpu.CompilerParams(
            collective_id=1, has_side_effects=True, vmem_limit_bytes=LIMIT
        ),
        name="attention_back_and_sum",
    )(valid, w, s, x, ga, mc, st, qkv, dq, g, gm, v)


def unpack_kernel(a_ref, b_ref, h_ref, m_ref, e_ref, r_ref):
    depth, width = m_ref.shape
    h_ref[...] = b_ref[:, : 3 * width].astype(f32)
    m_ref[...] = b_ref[:, 3 * width :].astype(f32)
    e_ref[...] = a_ref[:, : 4 * width].astype(f32)
    for j in range(4):
        lo = (4 + j) * width
        r_ref[j * depth : (j + 1) * depth, :] = a_ref[:, lo : lo + width].astype(f32)


def unpack_call(a, b):
    depth, width = a.shape[0], a.shape[1] // 8
    shape = jax.ShapeDtypeStruct
    vmem = pl.BlockSpec(memory_space=VMEM)
    return pl.pallas_call(
        unpack_kernel,
        out_shape=[
            shape((depth, 3 * width), f32), shape((depth, width), f32),
            shape((depth, 4 * width), f32), shape((4 * depth, width), f32),
        ],
        in_specs=[vmem] * 2,
        out_specs=[vmem] * 4,
        compiler_params=pltpu.CompilerParams(vmem_limit_bytes=LIMIT),
        name="unpack",
    )(a, b)


def on_device(
    image_tokens, valid_count, first_gain, first_bias, heads_weight, heads_bias,
    mixing_weight, mixing_bias, second_gain, second_bias, expand_weight, expand_bias,
    reduce_weight, reduce_bias, output_cotangent,
):
    _, span, width = image_tokens.shape
    depth = heads_weight.shape[0]
    padded = up(span, 16)
    z = lax.axis_index("grp")

    def pad_rows(x):
        return jnp.pad(x[0], ((0, padded - span), (0, 0)))

    x = pad_rows(image_tokens)
    oc = pad_rows(output_cotangent)
    ones = jnp.stack([first_gain, first_bias, mixing_bias, second_gain, second_bias, reduce_bias])
    col = jnp.arange(width) // depth == z
    rows6 = jnp.where(col[None, :], jnp.tile(ones, (1, 4)), 0)
    twos = jnp.where(jnp.arange(2 * width) // (2 * depth) == z, jnp.tile(heads_bias, 4), 0)
    fours = jnp.where(jnp.arange(4)[:, None] == z, expand_bias[None, :], 0)
    s = jnp.concatenate(
        [rows6, twos.reshape(2, width), fours, jnp.zeros((ROWS - 12, width), bf16)], 0
    ).astype(bf16)

    weights = (heads_weight, mixing_weight, expand_weight, reduce_weight)
    out, ga, g, gm, v, mc, st, qkv, dq, w_all, s_all = first_call(
        span, valid_count, weights, x, s, oc
    )
    ig, ga_sum, gb_sum, v = second_call(
        span, valid_count, w_all, s_all, x, ga, mc, st, qkv, dq, g, gm, v
    )
    teams = lax.axis_size("rep") // TEAM
    if teams > 1:
        ga_sum, gb_sum, v = lax.psum(
            (ga_sum.astype(f32) / TEAM, gb_sum.astype(f32) / TEAM, v / TEAM), "rep"
        )
    g_heads, g_mix, g_exp, g_red = unpack_call(ga_sum, gb_sum)
    six = lax.dynamic_slice(v, (0, z * depth), (6, depth))
    two = lax.dynamic_slice(v[6:8].reshape(2 * width), (z * 2 * depth,), (2 * depth,))
    four = lax.dynamic_slice(v, (8 + z, 0), (1, width))[0]
    return (
        out[None, :span], ig[None, :span],
        six[0], six[1], g_heads, two, g_mix, six[2], six[3], six[4],
        g_exp, four, g_red, six[5],
    )


def solution(mesh):
    tokens = P("rep", "grp", None)
    vec, mat = P("grp"), P("grp", None)
    weights = (vec, vec, mat, vec, mat, vec, vec, vec, mat, vec, mat, vec)
    return jax.shard_map(
        on_device,
        mesh=mesh,
        in_specs=(tokens, P("rep")) + weights + (tokens,),
        out_specs=(tokens, tokens) + weights,
        check_vma=False,
    )
```
